256 devices in a mesh: dp: 16 (over y, z_hi), vocab: 16 (over x, z_lo, core).
Axes of the slice: x: 4, y: 4, z: 8 (z_hi: 4, z_lo: 2; z = z_hi * 2 + z_lo), core: 2. Of those that a mesh axis runs over, the one named last changes fastest.
Arguments:
- teacher_rows: bfloat16 [512, 4608], P('dp', 'vocab'), may hold values from -40 to 40
- student_rows: bfloat16 [512, 3584], P('dp', 'vocab'), may hold values from -40 to 40
- teacher_gain: bfloat16 [4608], P('vocab'), may hold values from 0.099609375 to 1.8984375
- student_gain: bfloat16 [3584], P('vocab'), may hold values from 0.099609375 to 1.8984375
- teacher_head: bfloat16 [4608, 131072], P(None, ('dp', 'vocab')), may hold values from -0.25 to 0.25
- student_head: bfloat16 [3584, 131072], P(None, ('dp', 'vocab')), may hold values from -0.3125 to 0.3125
- labels: int32 [512], replicated, may hold values from 0 to 131071
Outputs:
- mean_loss: float32 [], replicated
- head_grad: bfloat16 [3584, 131072], P(None, ('dp', 'vocab'))
- gain_grad: float32 [3584], P('vocab')
- rows_grad: float32 [512, 3584], P('dp', 'vocab')
The draws below stay inside these ranges and needn't reach their ends.
All inputs are finite; a program needn't handle non-finite values.
Results may differ from the reference program's by a relative error of at most 0.0074.
Values may be sent and summed in bfloat16 or wider, within the bound.
A program may use at most 128 MiB of HBM per device.

```python
import math
import jax
import jax.numpy as jnp
import numpy as np
from jax import lax

DT = 4608
DS = 3584
TOKENS = 512
VOCAB = 131072


def log_spread(key, shape, lower, upper):
    return jnp.exp(jax.random.uniform(key, shape, jnp.float32, jnp.log(lower), jnp.log(upper)))


def draw_teacher_rows(key, part):
    key = jax.random.fold_in(key, 11)
    base_key, row_key, column_key = jax.random.split(key, 3)
    base = jnp.clip(jax.random.normal(base_key, (TOKENS, DT), jnp.float32), -4.0, 4.0)
    row_scale = log_spread(row_key, (TOKENS, 1), 0.5, 5.0)
    column_scale = log_spread(column_key, (1, DT), 0.5, 2.0)
    return (base * row_scale * column_scale).astype(jnp.bfloat16)


def draw_student_rows(key, part):
    key = jax.random.fold_in(key, 12)
    base_key, row_key, column_key = jax.random.split(key, 3)
    base = jnp.clip(jax.random.normal(base_key, (TOKENS, DS), jnp.float32), -4.0, 4.0)
    row_scale = log_spread(row_key, (TOKENS, 1), 0.5, 5.0)
    column_scale = log_spread(column_key, (1, DS), 0.5, 2.0)
    return (base * row_scale * column_scale).astype(jnp.bfloat16)


def place_ends(entries, stream_key, least, top_value):
    dims = entries.shape
    place = [jax.random.randint(jax.random.fold_in(stream_key, axis), (), 0, dims[axis]) for axis in range(len(dims))]
    entries = entries.at[tuple(place)].set(least)
    longest = dims.index(max(dims))
    place[longest] = (place[longest] + 1) % dims[longest]
    return entries.at[tuple(place)].set(top_value)


def levels(stream_key, shape, cuts, least, high):
    gain, own = 1.0, jax.random.fold_in(stream_key, 6)
    for axis_at, parts in cuts:
        draws = jnp.exp(jax.random.uniform(jax.random.fold_in(own, axis_at), (parts,), jnp.float32, least / len(cuts), high / len(cuts)))
        gain = gain * jnp.repeat(draws, shape[axis_at] // parts).reshape([-1 if axis == axis_at else 1 for axis in range(len(shape))])
    return gain


def wide_ids(key, shape, amount, skew):
    weights = [min(1 << octave, amount + 1 - (1 << octave)) * (1 << 20) // math.isqrt((1 << octave) ** skew) + 1 for octave in range((amount + 1).bit_length()) if 1 << octave <= amount]
    scale = 1 + sum(weights) // (1 << 30)
    listing = np.cumsum(np.array([max(1, weight // scale) for weight in weights]))
    ticket = jax.random.randint(jax.random.fold_in(key, 1), shape, 0, int(listing[len(weights) - 1]))
    start = jnp.left_shift(1, jnp.searchsorted(jnp.asarray(listing, jnp.int32), ticket, side="right").astype(jnp.int32))
    standing = start - 1 + jax.random.randint(jax.random.fold_in(key, 4), shape, 0, 1 << 30) % jnp.minimum(start, amount + 1 - start)
    return jax.random.permutation(jax.random.fold_in(key, 2), amount)[standing].astype(jnp.int32)


def scatter_about(stream_key, shape, spread, most, cuts=(), dtype=jnp.bfloat16):
    values = jax.random.normal(stream_key, shape, jnp.float32) * spread
    if len(cuts) > 0:
        values = levels(stream_key, shape, cuts, -0.22, 0.18) * values
    return jnp.clip(values, min=-most, max=most).astype(dtype)


def setup_inputs(seed: int = 0) -> dict:
    splits = jax.random.split(jax.random.key(seed), 8)
    teacher_rows = draw_teacher_rows(jax.random.fold_in(splits[7], 71), 0)
    student_rows = draw_student_rows(jax.random.fold_in(splits[7], 71), 0)
    teacher_gain = jnp.clip(1.0 + 0.18 * jax.random.normal(splits[2], (DT,), jnp.float32), 0.099609375, 1.8984375).astype(jnp.bfloat16)
    student_gain = jnp.clip(1.0 + 0.18 * jax.random.normal(splits[3], (DS,), jnp.float32), 0.099609375, 1.8984375).astype(jnp.bfloat16)
    teacher_head = scatter_about(splits[4], (DT, VOCAB), (DT // 9) ** -0.5, 0.25, ((1, 256),))
    student_head = scatter_about(splits[5], (DS, VOCAB), (DS // 9) ** -0.5, 0.3125, ((1, 256),))
    labels = place_ends(wide_ids(splits[6], (TOKENS,), VOCAB, 2), jax.random.fold_in(splits[6], 3), 0, VOCAB - 1).astype(jnp.int32)
    return {"teacher_rows": teacher_rows, "student_rows": student_rows, "teacher_gain": teacher_gain, "student_gain": student_gain, "teacher_head": teacher_head, "student_head": student_head, "labels": labels}


SOFT_CAP = 30.0
LABEL_WEIGHT = 0.5
LOSS_SCALE = 4096.0
NORM_EPS = 1e-06

def inverse_rms(values):
    return lax.rsqrt(lax.optimization_barrier(jnp.mean(values * values, axis=1, keepdims=True)) + NORM_EPS)

def capped(normed, head):
    return SOFT_CAP * jnp.tanh(jnp.dot(normed, head, preferred_element_type=jnp.float32) / SOFT_CAP)

def reference(teacher_rows, student_rows, teacher_gain, student_gain, teacher_head, student_head, labels):
    teacher_full = teacher_rows.astype(jnp.float32)
    student_full = student_rows.astype(jnp.float32)
    student_inv = inverse_rms(student_full)
    gain_wide = student_gain.astype(jnp.float32)
    teacher_norm = (teacher_full * inverse_rms(teacher_full) * teacher_gain.astype(jnp.float32)).astype(jnp.bfloat16)
    student_norm = (student_full * student_inv * gain_wide).astype(jnp.bfloat16)
    teacher_logit = capped(teacher_norm, teacher_head)
    student_logit = capped(student_norm, student_head)
    teacher_exp = jnp.exp(teacher_logit)
    student_exp = jnp.exp(student_logit)
    teacher_total = lax.optimization_barrier(jnp.sum(teacher_exp, axis=1))
    student_total = lax.optimization_barrier(jnp.sum(student_exp, axis=1))
    cross_sum = lax.optimization_barrier(jnp.sum(teacher_exp * (teacher_logit - student_logit), axis=1))
    columns = lax.broadcasted_iota(jnp.int32, student_logit.shape, 1)
    label_hit = (columns == labels.astype(jnp.int32)[:, None]).astype(jnp.float32)
    picked = lax.optimization_barrier(jnp.sum(label_hit * student_logit, axis=1))
    student_log = jnp.log(student_total)
    token_loss = cross_sum / teacher_total - jnp.log(teacher_total) + student_log + LABEL_WEIGHT * (student_log - picked)
    mean_loss = jnp.mean(token_loss)
    slope = 1.0 - (student_logit / SOFT_CAP) ** 2
    grad_logit = (LOSS_SCALE * ((1.0 + LABEL_WEIGHT) * student_exp / student_total[:, None] - teacher_exp / teacher_total[:, None] - LABEL_WEIGHT * label_hit) * slope).astype(jnp.bfloat16)
    head_grad = lax.dot_general(student_norm, grad_logit, (((0,), (0,)), ((), ())), preferred_element_type=jnp.float32).astype(jnp.bfloat16)
    norm_grad = lax.dot_general(grad_logit, student_head, (((1,), (1,)), ((), ())), preferred_element_type=jnp.float32)
    gain_grad = lax.optimization_barrier(jnp.sum(norm_grad * student_full * student_inv, axis=0))
    scaled_grad = norm_grad * gain_wide
    inner = lax.optimization_barrier(jnp.mean(scaled_grad * student_full, axis=1, keepdims=True))
    rows_grad = student_inv * scaled_grad - student_full * student_inv ** 3 * inner
    return (mean_loss, head_grad, gain_grad, rows_grad)
```

```python
import functools

import jax
import jax.numpy as jnp
from jax import lax
from jax.experimental import pallas as pl
from jax.experimental.pallas import tpu as pltpu
from jax.sharding import PartitionSpec as P

MESH = pl.DeviceIdType.MESH
F32 = jnp.float32
BF16 = jnp.bfloat16
DT = 4608
DS = 3584
TOKENS = 512
CAP = 30.0
SCALE = 4096.0
EPS = 1e-06
WT = 288
WS = 224
NSEM = 160


def row_iota(shape):
    return lax.broadcasted_iota(jnp.int32, shape, 0)


def lane_iota(shape):
    return lax.broadcasted_iota(jnp.int32, shape, 1)


def kernel(
    tr, sr, tg, sg, lab, th, sh,
    loss_o, gain_o, rows_o, hg_o,
    G, TA, TB, SP, accT, accS, accA, NT, NS, gl, HG,
    AT, AS, INVT, INVS, ST, LAB, SQ,
    MZ, MC, MX, MY, TC, TX, TY, TZ,
    PS, PR, R, RH, RB, Q, QR, W, ZR, NG,
    FY, FZ, IX, IZ, IC,
    hsem, osem, ssem, rsem,
):
    dp = lax.axis_index("dp")
    vo = lax.axis_index("vocab")
    y, zh = dp // 4, dp % 4
    x, zl, c = vo // 4, (vo // 2) % 2, vo % 2
    z = zh * 2 + zl
    zz = zl * 4 + zh
    pc = 1 - c

    def dev(x_, y_, z_, c_):
        return (y_ * 4 + z_ // 2, x_ * 4 + (z_ % 2) * 2 + c_)

    def m4(v):
        return lax.rem(v + 8, 4)

    def m8(v):
        return lax.rem(v + 16, 8)

    def at_x(d):
        return dev(m4(x + d), y, z, c)

    def at_y(d):
        return dev(x, m4(y + d), z, c)

    def at_z(d):
        return dev(x, y, m8(z + d), c)

    partner = dev(x, y, z, pc)

    def zidx(z_):
        return (z_ % 2) * 4 + z_ // 2

    count = [0]
    sent = []

    def send(src, dst, device):
        n = count[0]
        count[0] += 1
        cp = pltpu.make_async_remote_copy(
            src_ref=src, dst_ref=dst, send_sem=ssem.at[n], recv_sem=rsem.at[n],
            device_id=device, device_id_type=MESH,
        )
        cp.start()
        sent.append(cp)
        return n

    def recv(n, landing):
        pltpu.make_async_remote_copy(
            src_ref=landing, dst_ref=landing, send_sem=ssem.at[n], recv_sem=rsem.at[n],
            device_id=partner, device_id_type=MESH,
        ).wait_recv()

    def head_copies(v):
        v = jnp.int32(v)
        return (
            pltpu.make_async_copy(th.at[pl.ds(pl.multiple_of(v * WT, 16), 256)], TA.at[v], hsem.at[0, v]),
            pltpu.make_async_copy(th.at[pl.ds(pl.multiple_of(v * WT + 256, 16), 32)], TB.at[v, pl.ds(0, 32)], hsem.at[1, v]),
            pltpu.make_async_copy(sh.at[pl.ds(pl.multiple_of(v * WS, 16), WS)], SP.at[v, pl.ds(32, WS)], hsem.at[2, v]),
        )

    def start_heads(v, _):
        for cp in head_copies(v):
            cp.start()
        return 0

    lax.fori_loop(0, 16, start_heads, 0)

    def wait_heads(v, _):
        for cp in head_copies(v):
            cp.wait()
        return 0

    barrier = pltpu.get_barrier_semaphore()
    others = [partner] + [at_x(d) for d in (1, 2, 3)] + [at_y(d) for d in (1, 2, 3)] + [at_z(d) for d in range(1, 8)]
    for d in others:
        pl.semaphore_signal(barrier, inc=1, device_id=d, device_id_type=MESH)

    AT[...] = jnp.zeros_like(AT)
    AS[...] = jnp.zeros_like(AS)
    AT[0:32, 0:WT] = tr[...].astype(F32)
    AS[0:32, 0:WS] = sr[...].astype(F32)
    AT[32:40, 0:WT] = jnp.broadcast_to(tg[...].astype(F32), (8, WT))
    AS[32:40, 0:WS] = jnp.broadcast_to(sg[...].astype(F32), (8, WS))
    a_t = AT[...]
    a_s = pltpu.roll(AS[...], 32, 1)
    AS[...] = a_s
    tiles = [a_t[:, 0:128], a_t[:, 128:256], a_t[:, 256:384] + a_s[:, 0:128], a_s[:, 128:256]]
    for j in range(4):
        b, o = (x, y) if j < 2 else (y, x)
        G[j, b, c, o, zz] = tiles[j][0:32].astype(BF16)
    sq_t = jnp.sum(a_t[0:32] * a_t[0:32], axis=1, keepdims=True)
    sq_s = jnp.sum(a_s[0:32] * a_s[0:32], axis=1, keepdims=True)
    sub, lane = row_iota((32, 128)), lane_iota((32, 128))
    MZ[zz] = jnp.zeros((8, 128), F32)
    MZ[zz, 0:1] = jnp.sum(jnp.where(lane == sub, sq_t, 0.0) + jnp.where(lane == sub + 32, sq_s, 0.0), axis=0, keepdims=True)
    for j in range(4):
        MZ[zz, 4 + j : 5 + j] = tiles[j][32:33]

    TB[:, 32:128, :] = jnp.zeros((16, 96, 512), BF16)
    SP[:, 0:32, :] = jnp.zeros((16, 32, 512), BF16)

    pl.semaphore_wait(barrier, len(others))

    mz = [send(MZ.at[zz], MZ.at[zz], at_z(d)) for d in range(1, 8)]
    zs = {}
    for j in (0, 2, 1, 3):
        b, o = (x, y) if j < 2 else (y, x)
        piece = G.at[j, b, c, o, zz]
        zs[j] = [send(piece, piece, at_z(d)) for d in range(1, 8)]
    for d in range(1, 8):
        recv(mz[d - 1], MZ.at[zidx(m8(z - d))])
    MC[c] = jnp.zeros((16, 128), F32)
    for h in range(4):
        MC[c, h : h + 1] = MZ[h, 0:1] + MZ[4 + h, 0:1]
    MC[c, 8:12] = MZ[zh, 4:8]
    MC[c, 12:16] = MZ[4 + zh, 4:8]
    mc = send(MC.at[c], MC.at[c], partner)
    os = {}
    for j in (0, 2, 1, 3):
        b, o = (x, y) if j < 2 else (y, x)
        at_o = at_y if j < 2 else at_x
        for d in range(1, 8):
            recv(zs[j][d - 1], G.at[j, b, c, o, zidx(m8(z - d))])
        os[j] = [send(G.at[j, b, c, o], G.at[j, b, c, o], at_o(d)) for d in (1, 2, 3)]
    recv(mc, MC.at[pc])
    MX[x] = jnp.zeros((24, 128), F32)
    MX[x, 0:8] = MC[0, 0:8] + MC[1, 0:8]
    MX[x, 8:16] = MC[0, 8:16]
    MX[x, 16:24] = MC[1, 8:16]
    mx = [send(MX.at[x], MX.at[x], at_x(d)) for d in (1, 2, 3)]
    bs, ds = {}, {}
    for j in (0, 2, 1, 3):
        b, o = (x, y) if j < 2 else (y, x)
        at_b = at_x if j < 2 else at_y
        for d in (1, 2, 3):
            recv(os[j][d - 1], G.at[j, b, c, m4(o - d)])
        block = G.at[j, b, c]
        bs[j] = [send(block, block, at_b(1)), send(block, block, at_b(-1))]
        ds[j] = [send(block, block, partner)]
    for d in (1, 2, 3):
        recv(mx[d - 1], MX.at[m4(x - d)])
    MY[y] = jnp.zeros((8, 128), F32)
    MY[y] = MX[0, 0:8] + MX[1, 0:8] + MX[2, 0:8] + MX[3, 0:8]
    my = [send(MY.at[y], MY.at[y], at_y(d)) for d in (1, 2, 3)]
    fs = {}
    for j in (0, 2, 1, 3):
        b, o = (x, y) if j < 2 else (y, x)
        at_b = at_x if j < 2 else at_y
        recv(bs[j][0], G.at[j, m4(b - 1), c])
        half = G.at[j, m4(b - 1), c, pl.ds(0, 2)]
        f0 = send(half, half, at_b(1))
        recv(bs[j][1], G.at[j, m4(b + 1), c])
        half = G.at[j, m4(b + 1), c, pl.ds(2, 2)]
        f1 = send(half, half, at_b(-1))
        fs[j] = (f0, f1)
        for e in (-1, 1):
            block = G.at[j, m4(b + e), c]
            ds[j].append(send(block, block, partner))
    for d in (1, 2, 3):
        recv(my[d - 1], MY.at[m4(y - d)])
    lane1 = lane_iota((8, 128))
    for yy in range(4):
        sums = MY[yy]
        inv = lax.rsqrt(jnp.where(lane1 < 32, sums / DT, sums / DS) + EPS)
        for h in range(4):
            wide = jnp.broadcast_to(inv[h : h + 1], (32, 128))
            base = (yy * 4 + h) * 32
            INVT[base : base + 32, :] = jnp.broadcast_to(jnp.sum(jnp.where(lane == sub, wide, 0.0), axis=1, keepdims=True), (32, 128))
            INVS[base : base + 32, :] = jnp.broadcast_to(jnp.sum(jnp.where(lane == sub + 32, wide, 0.0), axis=1, keepdims=True), (32, 128))
    sub2, lane2 = row_iota((128, 128)), lane_iota((128, 128))
    for blk in range(4):
        wide = jnp.broadcast_to(lab[blk : blk + 1, :].astype(F32), (128, 128))
        LAB[blk * 128 : blk * 128 + 128, :] = jnp.broadcast_to(jnp.sum(jnp.where(lane2 == sub2, wide, 0.0), axis=1, keepdims=True), (128, 128))
    for j in (0, 2, 1, 3):
        b, o = (x, y) if j < 2 else (y, x)
        far = m4(b + 2)
        recv(fs[j][0], G.at[j, far, c, pl.ds(0, 2)])
        recv(fs[j][1], G.at[j, far, c, pl.ds(2, 2)])
        ds[j].append(send(G.at[j, far, c], G.at[j, far, c], partner))
    for j in (0, 2, 1, 3):
        b = x if j < 2 else y
        for k, e in enumerate((0, -1, 1, 2)):
            recv(ds[j][k], G.at[j, m4(b + e), pc])

    def norm_t(v, _):
        x_, zl_, c_ = v // 4, (v // 2) % 2, v % 2
        for j in range(2):
            gain = MX[x_, pl.ds(8 + c_ * 8 + zl_ * 4 + j, 1)]
            for o_ in range(4):
                rows = G[j, x_, c_, o_, pl.ds(zl_ * 4, 4)].reshape(128, 128).astype(F32)
                r = rows * INVT[o_ * 128 : o_ * 128 + 128, :] * gain
                NT[v, o_ * 128 : o_ * 128 + 128, j * 128 : j * 128 + 128] = r.astype(BF16)
        return 0

    def norm_s(v, _):
        x_, zl_, c_ = v // 4, (v // 2) % 2, v % 2
        for j in range(2):
            gain = MX[x_, pl.ds(8 + c_ * 8 + zl_ * 4 + 2 + j, 1)]
            for y_ in range(4):
                rows = G[2 + j, y_, c_, x_, pl.ds(zl_ * 4, 4)].reshape(128, 128).astype(F32)
                inv = INVS[y_ * 128 : y_ * 128 + 128, :]
                if j == 0:
                    inv = jnp.where(lane2 < 32, INVT[y_ * 128 : y_ * 128 + 128, :], inv)
                NS[v, y_ * 128 : y_ * 128 + 128, j * 128 : j * 128 + 128] = (rows * inv * gain).astype(BF16)
        return 0

    lax.fori_loop(0, 16, norm_t, 0)
    lax.fori_loop(0, 16, norm_s, 0)
    lax.fori_loop(0, 16, wait_heads, 0)

    accT[...] = jnp.zeros_like(accT)
    accS[...] = jnp.zeros_like(accS)

    def logits(i, _):
        q, n = i // 2, i % 2
        cols = pl.ds(pl.multiple_of(n * 256, 256), 256)
        lt = jnp.concatenate([NT[q * 4 + u] for u in range(4)], axis=1)
        rt = jnp.concatenate([TA[q * 4 + u, :, cols] for u in range(4)], axis=0)
        ls = jnp.concatenate([NS[q * 4 + u] for u in range(4)], axis=1)
        rs = jnp.concatenate([SP[q * 4 + u, :, cols] for u in range(4)], axis=0)
        lb = jnp.concatenate([NS[q * 4 + u, :, 0:128] for u in range(4)], axis=1)
        rb = jnp.concatenate([TB[q * 4 + u, :, cols] for u in range(4)], axis=0)
        accT[:, cols] += jnp.dot(lt, rt, preferred_element_type=F32) + jnp.dot(lb, rb, preferred_element_type=F32)
        accS[:, cols] += jnp.dot(ls, rs, preferred_element_type=F32)
        return 0

    lax.fori_loop(0, 8, logits, 0)

    first = (dp * 16 + vo) * 512

    def stats(i, _):
        rows = pl.ds(pl.multiple_of(i * 64, 64), 64)
        tl = CAP * jnp.tanh(accT[rows, :] / CAP)
        sl = CAP * jnp.tanh(accS[rows, :] / CAP)
        et, es = jnp.exp(tl), jnp.exp(sl)
        want = LAB[rows, 0:1]
        hit = (lane_iota((64, 512)) + first).astype(F32) == want
        picked = jnp.sum(jnp.where(hit, sl, 0.0), axis=1, keepdims=True)
        cross = jnp.sum(et * (tl - sl), axis=1, keepdims=True)
        tot_t = jnp.sum(et, axis=1, keepdims=True)
        tot_s = jnp.sum(es, axis=1, keepdims=True)
        ln = lane_iota((64, 128))
        ST[rows, :] = jnp.where(ln == 0, tot_t, jnp.where(ln == 1, tot_s, jnp.where(ln == 2, cross, jnp.where(ln == 3, picked, 0.0))))
        slope = SCALE * (1.0 - (sl / CAP) ** 2)
        accA[rows, :] = 1.5 * es * slope
        accT[rows, :] = et * slope
        accS[rows, :] = jnp.where(hit, 0.5 * slope, 0.0)
        return 0

    lax.fori_loop(0, 8, stats, 0)
    for blk in range(4):
        t = jnp.transpose(ST[blk * 128 : blk * 128 + 128, :])
        for q in range(4):
            TC[c, q * 4 + blk : q * 4 + blk + 1] = t[q : q + 1]
    n = send(TC.at[c], TC.at[c], partner)
    recv(n, TC.at[pc])
    TX[x] = TC[0] + TC[1]
    ns = [send(TX.at[x], TX.at[x], at_x(d)) for d in (1, 2, 3)]
    for d in (1, 2, 3):
        recv(ns[d - 1], TX.at[m4(x - d)])
    TY[y] = TX[0] + TX[1] + TX[2] + TX[3]
    ns = [send(TY.at[y], TY.at[y], at_y(d)) for d in (1, 2, 3)]
    for d in (1, 2, 3):
        recv(ns[d - 1], TY.at[m4(y - d)])
    TZ[zz] = TY[0] + TY[1] + TY[2] + TY[3]
    ns = [send(TZ.at[zz], TZ.at[zz], at_z(d)) for d in range(1, 8)]
    for d in range(1, 8):
        recv(ns[d - 1], TZ.at[zidx(m8(z - d))])
    total = TZ[0]
    for i in range(1, 8):
        total = total + TZ[i]
    tt, ts, cr, pk = total[0:4], total[4:8], total[8:12], total[12:16]
    ls = jnp.log(ts)
    token_loss = cr / tt - jnp.log(tt) + ls + 0.5 * (ls - pk)
    loss_o[...] = jnp.sum(jnp.sum(token_loss, axis=1, keepdims=True), axis=0, keepdims=True) / TOKENS
    rec = 1.0 / total[0:8]
    SQ[...] = jnp.zeros_like(SQ)
    for blk in range(4):
        SQ[0:1, :] = rec[blk : blk + 1]
        SQ[1:2, :] = rec[4 + blk : 5 + blk]
        ST[blk * 128 : blk * 128 + 128, :] = jnp.transpose(SQ[...])

    def grads(i, _):
        rows = pl.ds(pl.multiple_of(i * 64, 64), 64)
        gl[rows, :] = (accA[rows, :] * ST[rows, 1:2] - accT[rows, :] * ST[rows, 0:1] - accS[rows, :]).astype(BF16)
        return 0

    lax.fori_loop(0, 8, grads, 0)

    def partial(v):
        return lax.dot_general(gl[...], SP[v], (((1,), (1,)), ((), ())), preferred_element_type=F32)

    def share_other(i, _):
        x_, zl_ = i // 2, i % 2
        out = partial(x_ * 4 + zl_ * 2 + pc).astype(BF16)
        for y_ in range(4):
            part = out[y_ * 128 : y_ * 128 + 128]
            PS[0, x_, y_, pl.ds(zl_ * 4, 4)] = part[:, 0:128].reshape(4, 32, 128)
            PS[1, y_, x_, pl.ds(zl_ * 4, 4)] = part[:, 128:256].reshape(4, 32, 128)
        return 0

    lax.fori_loop(0, 8, share_other, 0)
    ps = [send(PS.at[k], PR.at[k], partner) for k in range(2)]

    def share_own(i, _):
        x_, zl_ = i // 2, i % 2
        out = partial(x_ * 4 + zl_ * 2 + c).astype(BF16)
        for y_ in range(4):
            part = out[y_ * 128 : y_ * 128 + 128]
            R[0, x_, y_, pl.ds(zl_ * 4, 4)] = part[:, 0:128].reshape(4, 32, 128)
            R[1, y_, x_, pl.ds(zl_ * 4, 4)] = part[:, 128:256].reshape(4, 32, 128)
        return 0

    lax.fori_loop(0, 8, share_own, 0)

    def add_pair(i, k):
        b_, o_ = i // 4, i % 4
        R[k, b_, o_] = (R[k, b_, o_].astype(F32) + PR[k, b_, o_].astype(F32)).astype(BF16)
        return k

    r1 = {}
    for k in range(2):
        b = x if k == 0 else y
        at_b = at_x if k == 0 else at_y
        recv(ps[k], PR.at[k])
        lax.fori_loop(0, 16, add_pair, k)
        far = m4(b + 2)
        r1[k] = (
            send(R.at[k, far, pl.ds(0, 2)], RH.at[k, 0], at_b(1)),
            send(R.at[k, far, pl.ds(2, 2)], RH.at[k, 1], at_b(-1)),
        )

    def head_grad(v, _):
        out = lax.dot_general(NS[v], gl[...], (((0,), (0,)), ((), ())), preferred_element_type=F32)
        HG[pl.ds(pl.multiple_of(v * WS, 16), WS), :] = out[32:256].astype(BF16)
        return 0

    lax.fori_loop(0, 4, head_grad, 0)
    r2 = {}
    for k in range(2):
        b = x if k == 0 else y
        at_b = at_x if k == 0 else at_y
        recv(r1[k][0], RH.at[k, 0])
        for o_ in range(2):
            R[k, m4(b + 1), o_] = (R[k, m4(b + 1), o_].astype(F32) + RH[k, 0, o_].astype(F32)).astype(BF16)
        n0 = send(R.at[k, m4(b + 1)], RB.at[k, 0], at_b(1))
        recv(r1[k][1], RH.at[k, 1])
        for o_ in range(2):
            R[k, m4(b - 1), 2 + o_] = (R[k, m4(b - 1), 2 + o_].astype(F32) + RH[k, 1, o_].astype(F32)).astype(BF16)
        n1 = send(R.at[k, m4(b - 1)], RB.at[k, 1], at_b(-1))
        r2[k] = (n0, n1)
    lax.fori_loop(4, 16, head_grad, 0)
    out_copy = pltpu.make_async_copy(HG, hg_o, osem.at[0])
    out_copy.start()
    r3 = {}
    for k in range(2):
        b, o = (x, y) if k == 0 else (y, x)
        at_o = at_y if k == 0 else at_x
        recv(r2[k][0], RB.at[k, 0])
        recv(r2[k][1], RB.at[k, 1])
        for o_ in range(4):
            Q[k, o_] = (R[k, b, o_].astype(F32) + RB[k, 0, o_].astype(F32) + RB[k, 1, o_].astype(F32)).astype(BF16)
        r3[k] = [send(Q.at[k, m4(o + d)], QR.at[k, d - 1], at_o(d)) for d in (1, 2, 3)]
    r4 = {}
    for k in range(2):
        o = y if k == 0 else x
        for d in (1, 2, 3):
            recv(r3[k][d - 1], QR.at[k, d - 1])
        W[k] = (Q[k, o].astype(F32) + QR[k, 0].astype(F32) + QR[k, 1].astype(F32) + QR[k, 2].astype(F32)).astype(BF16)
        r4[k] = [send(W.at[k, zidx(m8(z + d))], ZR.at[k, d - 1], at_z(d)) for d in range(1, 8)]
    for k in range(2):
        for d in range(1, 8):
            recv(r4[k][d - 1], ZR.at[k, d - 1])
        got = W[k, zz].astype(F32)
        for d in range(7):
            got = got + ZR[k, d].astype(F32)
        NG[:, k * 128 : k * 128 + 128] = got

    own = pl.ds(pl.multiple_of(dp * 32, 32), 32)
    inv = INVS[own, 0:1]
    ng = NG[...]
    rows = AS[0:32, :]
    gain = AS[32:33, :]
    scaled = ng * gain
    FY[y] = jnp.broadcast_to(jnp.sum(ng * rows * inv, axis=0, keepdims=True), (8, 256))
    inner = jnp.sum(scaled * rows, axis=1, keepdims=True)
    IX[x] = jnp.broadcast_to(jnp.sum(jnp.where(lane == sub, inner, 0.0), axis=0, keepdims=True), (8, 128))
    fy = [send(FY.at[y], FY.at[y], at_y(d)) for d in (1, 2, 3)]
    ix = [send(IX.at[x], IX.at[x], at_x(d)) for d in (1, 2, 3)]
    for d in (1, 2, 3):
        recv(ix[d - 1], IX.at[m4(x - d)])
    IZ[zl] = IX[0] + IX[1] + IX[2] + IX[3]
    iz = send(IZ.at[zl], IZ.at[zl], dev(x, y, zh * 2 + 1 - zl, c))
    for d in (1, 2, 3):
        recv(fy[d - 1], FY.at[m4(y - d)])
    FZ[zh] = FY[0] + FY[1] + FY[2] + FY[3]
    fz = [send(FZ.at[zh], FZ.at[zh], at_z(2 * d)) for d in (1, 2, 3)]
    recv(iz, IZ.at[1 - zl])
    IC[c] = IZ[0] + IZ[1]
    ic = send(IC.at[c], IC.at[c], partner)
    recv(ic, IC.at[pc])
    wide = jnp.broadcast_to((IC[0] + IC[1])[0:1], (32, 128))
    inner = jnp.sum(jnp.where(lane == sub, wide, 0.0), axis=1, keepdims=True) / DS
    out = inv * scaled - rows * (inv * inv * inv) * inner
    rows_o[...] = pltpu.roll(out, 224, 1)[:, 0:WS]
    for d in (1, 2, 3):
        recv(fz[d - 1], FZ.at[m4(zh - d)])
    gain_o[...] = pltpu.roll(FZ[0] + FZ[1] + FZ[2] + FZ[3], 224, 1)[0:1, 0:WS]
    out_copy.wait()
    for cp in sent:
        cp.wait_send()


def local(teacher_rows, student_rows, teacher_gain, student_gain, teacher_head, student_head, labels):
    vmem = pl.BlockSpec(memory_space=pltpu.VMEM)
    anyw = pl.BlockSpec(memory_space=pl.ANY)
    V = pltpu.VMEM
    loss, gain_grad, rows_grad, head_grad = pl.pallas_call(
        kernel,
        out_shape=(
            jax.ShapeDtypeStruct((1, 1), F32),
            jax.ShapeDtypeStruct((1, WS), F32),
            jax.ShapeDtypeStruct((32, WS), F32),
            jax.ShapeDtypeStruct((DS, 512), BF16),
        ),
        in_specs=[vmem, vmem, vmem, vmem, vmem, anyw, anyw],
        out_specs=(vmem, vmem, vmem, anyw),
        scratch_shapes=[
            V((4, 4, 2, 4, 8, 32, 128), BF16),
            V((16, 256, 512), BF16),
            V((16, 128, 512), BF16),
            V((16, 256, 512), BF16),
            V((512, 512), F32), V((512, 512), F32), V((512, 512), F32),
            V((16, 512, 256), BF16), V((16, 512, 256), BF16),
            V((512, 512), BF16),
            V((DS, 512), BF16),
            V((40, 384), F32), V((40, 256), F32),
            V((512, 128), F32), V((512, 128), F32), V((512, 128), F32), V((512, 128), F32),
            V((128, 128), F32),
            V((8, 8, 128), F32), V((2, 16, 128), F32), V((4, 24, 128), F32), V((4, 8, 128), F32),
            V((2, 16, 128), F32), V((4, 16, 128), F32), V((4, 16, 128), F32), V((8, 16, 128), F32),
            V((2, 4, 4, 8, 32, 128), BF16), V((2, 4, 4, 8, 32, 128), BF16), V((2, 4, 4, 8, 32, 128), BF16),
            V((2, 2, 2, 8, 32, 128), BF16), V((2, 2, 4, 8, 32, 128), BF16),
            V((2, 4, 8, 32, 128), BF16), V((2, 3, 8, 32, 128), BF16),
            V((2, 8, 32, 128), BF16), V((2, 7, 32, 128), BF16),
            V((32, 256), F32),
            V((4, 8, 256), F32), V((4, 8, 256), F32),
            V((4, 8, 128), F32), V((2, 8, 128), F32), V((2, 8, 128), F32),
            pltpu.SemaphoreType.DMA((3, 16)),
            pltpu.SemaphoreType.DMA((1,)),
            pltpu.SemaphoreType.DMA((NSEM,)),
            pltpu.SemaphoreType.DMA((NSEM,)),
        ],
        compiler_params=pltpu.CompilerParams(
            collective_id=0, has_side_effects=True, vmem_limit_bytes=60 << 20
        ),
    )(
        teacher_rows, student_rows, teacher_gain.reshape(1, WT), student_gain.reshape(1, WS),
        labels.reshape(4, 128), teacher_head, student_head,
    )
    return loss.reshape(()), head_grad, gain_grad.reshape(WS), rows_grad


def solution(mesh):
    in_specs = (
        P("dp", "vocab"),
        P("dp", "vocab"),
        P("vocab"),
        P("vocab"),
        P(None, ("dp", "vocab")),
        P(None, ("dp", "vocab")),
        P(),
    )
    out_specs = (P(), P(None, ("dp", "vocab")), P("vocab"), P("dp", "vocab"))
    return jax.shard_map(local, mesh=mesh, in_specs=in_specs, out_specs=out_specs, check_vma=False)
```

```python
import functools

import jax
import jax.numpy as jnp
from jax import lax
from jax.experimental import pallas as pl
from jax.experimental.pallas import tpu as pltpu
from jax.sharding import PartitionSpec as P

MESH = pl.DeviceIdType.MESH
F32 = jnp.float32
BF16 = jnp.bfloat16
DT = 4608
DS = 3584
TOKENS = 512
CAP = 30.0
SCALE = 4096.0
EPS = 1e-06
WT = 288
WS = 224
NSEM = 160


def row_iota(shape):
    return lax.broadcasted_iota(jnp.int32, shape, 0)


def lane_iota(shape):
    return lax.broadcasted_iota(jnp.int32, shape, 1)


def kernel(
    tr, sr, tg, sg, lab, th, sh,
    loss_o, gain_o, rows_o, hg_o,
    G, TA, TB, SP, SPT, accT, accS, accA, NT, NS, gl, accZ,
    AT, AS, INVT, INVS, ST, LAB, SQ,
    MZ, MC, MX, MY, TC, TX, TY, TZ,
    PS, PR, R, RH, RB, Q, QR, W, ZR, NG,
    GI, GX, GXR, GY, GZ, GT,
    hsem, ssem, rsem,
):
    dp = lax.axis_index("dp")
    vo = lax.axis_index("vocab")
    y, zh = dp // 4, dp % 4
    x, zl, c = vo // 4, (vo // 2) % 2, vo % 2
    z = zh * 2 + zl
    zz = zl * 4 + zh
    pc = 1 - c

    def dev(x_, y_, z_, c_):
        return (y_ * 4 + z_ // 2, x_ * 4 + (z_ % 2) * 2 + c_)

    def m4(v):
        return lax.rem(v + 8, 4)

    def m8(v):
        return lax.rem(v + 16, 8)

    def at_x(d):
        return dev(m4(x + d), y, z, c)

    def at_y(d):
        return dev(x, m4(y + d), z, c)

    def at_z(d):
        return dev(x, y, m8(z + d), c)

    partner = dev(x, y, z, pc)

    def zidx(z_):
        return (z_ % 2) * 4 + z_ // 2

    count = [0]
    sent = []

    def send(src, dst, device):
        n = count[0]
        count[0] += 1
        cp = pltpu.make_async_remote_copy(
            src_ref=src, dst_ref=dst, send_sem=ssem.at[n], recv_sem=rsem.at[n],
            device_id=device, device_id_type=MESH,
        )
        cp.start()
        sent.append(cp)
        return n

    def recv(n, landing):
        pltpu.make_async_remote_copy(
            src_ref=landing, dst_ref=landing, send_sem=ssem.at[n], recv_sem=rsem.at[n],
            device_id=partner, device_id_type=MESH,
        ).wait_recv()

    def head_copies(v):
        v = jnp.int32(v)
        return (
            pltpu.make_async_copy(th.at[pl.ds(pl.multiple_of(v * WT, 16), 256)], TA.at[v], hsem.at[0, v]),
            pltpu.make_async_copy(th.at[pl.ds(pl.multiple_of(v * WT + 256, 16), 32)], TB.at[v, pl.ds(0, 32)], hsem.at[1, v]),
            pltpu.make_async_copy(sh.at[pl.ds(pl.multiple_of(v * WS, 16), WS)], SP.at[v, pl.ds(32, WS)], hsem.at[2, v]),
        )

    def wait_heads(v, _):
        for cp in head_copies(v):
            cp.wait()
        return 0

    barrier = pltpu.get_barrier_semaphore()
    others = [partner] + [at_x(d) for d in (1, 2, 3)] + [at_y(d) for d in (1, 2, 3)] + [at_z(d) for d in range(1, 8)]
    for d in others:
        pl.semaphore_signal(barrier, inc=1, device_id=d, device_id_type=MESH)

    AT[...] = jnp.zeros_like(AT)
    AS[...] = jnp.zeros_like(AS)
    AT[0:32, 0:WT] = tr[...].astype(F32)
    AS[0:32, 0:WS] = sr[...].astype(F32)
    AT[32:40, 0:WT] = jnp.broadcast_to(tg[...].astype(F32).reshape(1, WT), (8, WT))
    AS[32:40, 0:WS] = jnp.broadcast_to(sg[...].astype(F32).reshape(1, WS), (8, WS))
    a_t = AT[...]
    a_s = pltpu.roll(AS[...], 32, 1)
    AS[...] = a_s
    tiles = [a_t[:, 0:128], a_t[:, 128:256], a_t[:, 256:384] + a_s[:, 0:128], a_s[:, 128:256]]
    for j in range(4):
        b, o = (x, y) if j < 2 else (y, x)
        G[j, b, c, o, zz] = tiles[j][0:32].astype(BF16)
    sq_t = jnp.sum(a_t[0:32] * a_t[0:32], axis=1, keepdims=True)
    sq_s = jnp.sum(a_s[0:32] * a_s[0:32], axis=1, keepdims=True)
    sub, lane = row_iota((32, 128)), lane_iota((32, 128))
    MZ[zz] = jnp.zeros((8, 128), F32)
    MZ[zz, 0:1] = jnp.sum(jnp.where(lane == sub, sq_t, 0.0) + jnp.where(lane == sub + 32, sq_s, 0.0), axis=0, keepdims=True)
    for j in range(4):
        MZ[zz, 4 + j : 5 + j] = tiles[j][32:33]

    pl.semaphore_wait(barrier, len(others))

    mz = [send(MZ.at[zz], MZ.at[zz], at_z(d)) for d in range(1, 8)]
    zs = {}
    for j in (0, 2, 1, 3):
        b, o = (x, y) if j < 2 else (y, x)
        piece = G.at[j, b, c, o, zz]
        zs[j] = [send(piece, piece, at_z(d)) for d in range(1, 8)]

    def start_heads(v, _):
        for cp in head_copies(v):
            cp.start()
        return 0

    lax.fori_loop(0, 16, start_heads, 0)
    TB[:, 32:128, :] = jnp.zeros((16, 96, 512), BF16)
    SP[:, 0:32, :] = jnp.zeros((16, 32, 512), BF16)
    accT[...] = jnp.zeros_like(accT)
    accS[...] = jnp.zeros_like(accS)

    def axes(j):
        return (x, y, at_x, at_y) if j < 2 else (y, x, at_y, at_x)

    o1, o2, b1, b2, ds = {}, {}, {}, {}, {}

    def z_done(j):
        b, o, at_b, at_o = axes(j)
        for d in range(1, 8):
            recv(zs[j][d - 1], G.at[j, b, c, o, zidx(m8(z - d))])
        block = G.at[j, b, c, o]
        if j in (0, 2):
            o1[j] = [send(block, block, at_o(d)) for d in (1, 2, 3)]
        else:
            o1[j] = [send(block, block, at_o(1)), send(block, block, at_o(-1))]

    def o_near(j):
        b, o, at_b, at_o = axes(j)
        recv(o1[j][0], G.at[j, b, c, m4(o - 1)])
        half = G.at[j, b, c, m4(o - 1), pl.ds(0, 4)]
        f0 = send(half, half, at_o(1))
        recv(o1[j][1], G.at[j, b, c, m4(o + 1)])
        half = G.at[j, b, c, m4(o + 1), pl.ds(4, 4)]
        o2[j] = [f0, send(half, half, at_o(-1))]

    def o_far(j):
        b, o, at_b, at_o = axes(j)
        if j in (0, 2):
            for d in (1, 2, 3):
                recv(o1[j][d - 1], G.at[j, b, c, m4(o - d)])
        else:
            recv(o2[j][0], G.at[j, b, c, m4(o + 2), pl.ds(0, 4)])
            recv(o2[j][1], G.at[j, b, c, m4(o + 2), pl.ds(4, 4)])
        block = G.at[j, b, c]
        b1[j] = [send(block, block, at_b(1)), send(block, block, at_b(-1))]
        ds[j] = [send(block, block, partner)]

    def b_near(j):
        b, o, at_b, at_o = axes(j)
        recv(b1[j][0], G.at[j, m4(b - 1), c])
        half = G.at[j, m4(b - 1), c, pl.ds(0, 2)]
        f0 = send(half, half, at_b(1))
        recv(b1[j][1], G.at[j, m4(b + 1), c])
        half = G.at[j, m4(b + 1), c, pl.ds(2, 2)]
        b2[j] = [f0, send(half, half, at_b(-1))]
        for e in (-1, 1):
            block = G.at[j, m4(b + e), c]
            ds[j].append(send(block, block, partner))

    def b_far(j):
        b, o, at_b, at_o = axes(j)
        far = m4(b + 2)
        recv(b2[j][0], G.at[j, far, c, pl.ds(0, 2)])
        recv(b2[j][1], G.at[j, far, c, pl.ds(2, 2)])
        ds[j].append(send(G.at[j, far, c], G.at[j, far, c], partner))

    def core_done(j, ks):
        b = x if j < 2 else y
        for k in ks:
            recv(ds[j][k], G.at[j, m4(b + (0, -1, 1, 2)[k]), pc])

    for d in range(1, 8):
        recv(mz[d - 1], MZ.at[zidx(m8(z - d))])
    MC[c] = jnp.zeros((16, 128), F32)
    for h in range(4):
        MC[c, h : h + 1] = MZ[h, 0:1] + MZ[4 + h, 0:1]
    MC[c, 8:12] = MZ[zh, 4:8]
    MC[c, 12:16] = MZ[4 + zh, 4:8]
    mc = send(MC.at[c], MC.at[c], partner)
    z_done(0)
    z_done(2)
    recv(mc, MC.at[pc])
    MX[x] = jnp.zeros((24, 128), F32)
    MX[x, 0:8] = MC[0, 0:8] + MC[1, 0:8]
    MX[x, 8:16] = MC[0, 8:16]
    MX[x, 16:24] = MC[1, 8:16]
    mx = [send(MX.at[x], MX.at[x], at_x(d)) for d in (1, 2, 3)]
    z_done(1)
    z_done(3)
    for d in (1, 2, 3):
        recv(mx[d - 1], MX.at[m4(x - d)])
    MY[y] = MX[0, 0:8] + MX[1, 0:8] + MX[2, 0:8] + MX[3, 0:8]
    my = [send(MY.at[y], MY.at[y], at_y(d)) for d in (1, 2, 3)]
    o_far(0)
    o_near(1)
    o_far(2)
    o_near(3)
    o_far(1)
    o_far(3)
    for d in (1, 2, 3):
        recv(my[d - 1], MY.at[m4(y - d)])
    lane1 = lane_iota((8, 128))
    for yy in range(4):
        sums = MY[yy]
        inv = lax.rsqrt(jnp.where(lane1 < 32, sums / DT, sums / DS) + EPS)
        for h in range(4):
            wide = jnp.broadcast_to(inv[h : h + 1], (32, 128))
            base = (yy * 4 + h) * 32
            INVT[base : base + 32, :] = jnp.broadcast_to(jnp.sum(jnp.where(lane == sub, wide, 0.0), axis=1, keepdims=True), (32, 128))
            INVS[base : base + 32, :] = jnp.broadcast_to(jnp.sum(jnp.where(lane == sub + 32, wide, 0.0), axis=1, keepdims=True), (32, 128))
    sub2, lane2 = row_iota((128, 128)), lane_iota((128, 128))
    for blk in range(4):
        wide = jnp.broadcast_to(lab[blk : blk + 1, :].astype(F32), (128, 128))
        LAB[blk * 128 : blk * 128 + 128, :] = jnp.broadcast_to(jnp.sum(jnp.where(lane2 == sub2, wide, 0.0), axis=1, keepdims=True), (128, 128))
    lax.fori_loop(0, 16, wait_heads, 0)

    def teacher_block(x_):
        def norm(u, _):
            zl_, c_ = u // 2, u % 2
            for j in range(2):
                gain = MX[x_, pl.ds(8 + c_ * 8 + zl_ * 4 + j, 1)]
                for o_ in range(4):
                    rows = G[j, x_, c_, o_, pl.ds(zl_ * 4, 4)].reshape(128, 128).astype(F32)
                    r = rows * INVT[o_ * 128 : o_ * 128 + 128, :] * gain
                    NT[u, o_ * 128 : o_ * 128 + 128, j * 128 : j * 128 + 128] = r.astype(BF16)
            return 0

        lax.fori_loop(0, 4, norm, 0)

        def mul(n, _):
            cols = pl.ds(pl.multiple_of(n * 256, 256), 256)
            lt = jnp.concatenate([NT[u] for u in range(4)], axis=1)
            rt = jnp.concatenate([TA[x_ * 4 + u, :, cols] for u in range(4)], axis=0)
            accT[:, cols] += jnp.dot(lt, rt, preferred_element_type=F32)
            return 0

        lax.fori_loop(0, 2, mul, 0)

    def student_norm(y_):
        tok = pl.ds(pl.multiple_of(y_ * 128, 128), 128)

        def norm(v, _):
            x_, zl_, c_ = v // 4, (v // 2) % 2, v % 2
            for j in range(2):
                gain = MX[x_, pl.ds(8 + c_ * 8 + zl_ * 4 + 2 + j, 1)]
                rows = G[2 + j, y_, c_, x_, pl.ds(zl_ * 4, 4)].reshape(128, 128).astype(F32)
                inv = INVS[tok, :]
                if j == 0:
                    inv = jnp.where(lane2 < 32, INVT[tok, :], inv)
                NS[v, tok, j * 128 : j * 128 + 128] = (rows * inv * gain).astype(BF16)
            return 0

        lax.fori_loop(0, 16, norm, 0)

    def student_block(y_):
        tok = pl.ds(pl.multiple_of(y_ * 128, 128), 128)

        def mul(q, _):
            ls = jnp.concatenate([NS[q * 4 + u, tok, :] for u in range(4)], axis=1)
            rs = jnp.concatenate([SP[q * 4 + u] for u in range(4)], axis=0)
            lb = jnp.concatenate([NS[q * 4 + u, tok, 0:128] for u in range(4)], axis=1)
            rb = jnp.concatenate([TB[q * 4 + u] for u in range(4)], axis=0)
            accS[tok, :] += jnp.dot(ls, rs, preferred_element_type=F32)
            accT[tok, :] += jnp.dot(lb, rb, preferred_element_type=F32)
            return 0

        lax.fori_loop(0, 4, mul, 0)

    def flip(v, _):
        SPT[:, pl.ds(pl.multiple_of(v * 256, 256), 256)] = jnp.transpose(SP[v])
        return 0

    lax.fori_loop(0, 8, flip, 0)
    b_near(0)
    b_near(2)
    for j in range(4):
        core_done(j, (0,))
    teacher_block(x)
    b_near(1)
    b_near(3)
    student_norm(y)
    student_block(y)
    lax.fori_loop(8, 16, flip, 0)
    b_far(0)
    b_far(2)
    for j in range(4):
        core_done(j, (1, 2))

    def teacher_near(i, _):
        teacher_block(m4(x - 1 + 2 * i))
        return 0

    def student_near(i, _):
        y_ = m4(y - 1 + 2 * i)
        student_norm(y_)
        student_block(y_)
        return 0

    lax.fori_loop(0, 2, teacher_near, 0)
    b_far(1)
    b_far(3)
    lax.fori_loop(0, 2, student_near, 0)
    for j in range(4):
        core_done(j, (3,))
    teacher_block(m4(x + 2))
    student_norm(m4(y + 2))
    student_block(m4(y + 2))

    first = (dp * 16 + vo) * 512

    def stats(i, _):
        rows = pl.ds(pl.multiple_of(i * 64, 64), 64)
        tl = CAP * jnp.tanh(accT[rows, :] / CAP)
        sl = CAP * jnp.tanh(accS[rows, :] / CAP)
        et, es = jnp.exp(tl), jnp.exp(sl)
        want = LAB[rows, 0:1]
        hit = (lane_iota((64, 512)) + first).astype(F32) == want
        picked = jnp.sum(jnp.where(hit, sl, 0.0), axis=1, keepdims=True)
        cross = jnp.sum(et * (tl - sl), axis=1, keepdims=True)
        tot_t = jnp.sum(et, axis=1, keepdims=True)
        tot_s = jnp.sum(es, axis=1, keepdims=True)
        ln = lane_iota((64, 128))
        ST[rows, :] = jnp.where(ln == 0, tot_t, jnp.where(ln == 1, tot_s, jnp.where(ln == 2, cross, jnp.where(ln == 3, picked, 0.0))))
        accZ[rows, :] = accS[rows, :]
        slope = SCALE * (1.0 - (sl / CAP) ** 2)
        accA[rows, :] = 1.5 * es * slope
        accT[rows, :] = et * slope
        accS[rows, :] = jnp.where(hit, 0.5 * slope, 0.0)
        return 0

    lax.fori_loop(0, 8, stats, 0)
    for blk in range(4):
        t = jnp.transpose(ST[blk * 128 : blk * 128 + 128, :])
        for q in range(4):
            TC[c, q * 4 + blk : q * 4 + blk + 1] = t[q : q + 1]
    n = send(TC.at[c], TC.at[c], partner)
    recv(n, TC.at[pc])
    TX[x] = TC[0] + TC[1]
    ns = [send(TX.at[x], TX.at[x], at_x(d)) for d in (1, 2, 3)]
    for d in (1, 2, 3):
        recv(ns[d - 1], TX.at[m4(x - d)])
    TY[y] = TX[0] + TX[1] + TX[2] + TX[3]
    ns = [send(TY.at[y], TY.at[y], at_y(d)) for d in (1, 2, 3)]
    for d in (1, 2, 3):
        recv(ns[d - 1], TY.at[m4(y - d)])
    TZ[zz] = TY[0] + TY[1] + TY[2] + TY[3]
    ns = [send(TZ.at[zz], TZ.at[zz], at_z(d)) for d in range(1, 8)]
    for d in range(1, 8):
        recv(ns[d - 1], TZ.at[zidx(m8(z - d))])
    total = TZ[0]
    for i in range(1, 8):
        total = total + TZ[i]
    tt, ts, cr, pk = total[0:4], total[4:8], total[8:12], total[12:16]
    ls = jnp.log(ts)
    token_loss = cr / tt - jnp.log(tt) + ls + 0.5 * (ls - pk)
    loss_o[...] = jnp.sum(jnp.sum(token_loss, axis=1, keepdims=True), axis=0, keepdims=True) / TOKENS
    rec = 1.0 / total[0:8]
    SQ[...] = jnp.zeros_like(SQ)
    for blk in range(4):
        SQ[0:1, :] = rec[blk : blk + 1]
        SQ[1:2, :] = rec[4 + blk : 5 + blk]
        ST[blk * 128 : blk * 128 + 128, :] = jnp.transpose(SQ[...])

    def grads(i, _):
        rows = pl.ds(pl.multiple_of(i * 64, 64), 64)
        g = (accA[rows, :] * ST[rows, 1:2] - accT[rows, :] * ST[rows, 0:1] - accS[rows, :]).astype(BF16)
        gl[rows, :] = g
        dots = jnp.sum(g.astype(F32) * accZ[rows, :], axis=1, keepdims=True)
        LAB[rows, :] = jnp.broadcast_to(dots, (64, 128))
        return 0

    lax.fori_loop(0, 8, grads, 0)

    def as_row(column):
        return jnp.sum(jnp.where(lane2 == sub2, column, 0.0), axis=0, keepdims=True)

    def partial(v):
        return jnp.dot(gl[...], SPT[:, pl.ds(pl.multiple_of(v * 256, 256), 256)], preferred_element_type=F32).astype(BF16)

    def share(dst, x_, c_):
        def one(zl_, _):
            out = partial(x_ * 4 + zl_ * 2 + c_)
            for y_ in range(4):
                part = out[y_ * 128 : y_ * 128 + 128]
                dst[0, x_, y_, pl.ds(zl_ * 4, 4)] = part[:, 0:128].reshape(4, 32, 128)
                dst[1, y_, x_, pl.ds(zl_ * 4, 4)] = part[:, 128:256].reshape(4, 32, 128)
            return 0

        lax.fori_loop(0, 2, one, 0)

    order = [m4(x + 2), m4(x + 1), m4(x - 1), x]
    ps = []
    for x_ in order:
        share(PS, x_, pc)
        ps.append((send(PS.at[0, x_], PR.at[0, x_], partner), send(PS.at[1, :, x_], PR.at[1, :, x_], partner)))
    r1 = {}
    for i, x_ in enumerate(order):
        share(R, x_, c)
        recv(ps[i][0], PR.at[0, x_])
        for o_ in range(4):
            R[0, x_, o_] = (R[0, x_, o_].astype(F32) + PR[0, x_, o_].astype(F32)).astype(BF16)
        recv(ps[i][1], PR.at[1, :, x_])
        for b_ in range(4):
            R[1, b_, x_] = (R[1, b_, x_].astype(F32) + PR[1, b_, x_].astype(F32)).astype(BF16)
        if i == 0:
            r1[0] = (
                send(R.at[0, x_, pl.ds(0, 2)], RH.at[0, 0], at_x(1)),
                send(R.at[0, x_, pl.ds(2, 2)], RH.at[0, 1], at_x(-1)),
            )
    far = m4(y + 2)
    r1[1] = (
        send(R.at[1, far, pl.ds(0, 2)], RH.at[1, 0], at_y(1)),
        send(R.at[1, far, pl.ds(2, 2)], RH.at[1, 1], at_y(-1)),
    )

    def head_grad(v, _):
        out = lax.dot_general(NS[v], gl[...], (((0,), (0,)), ((), ())), preferred_element_type=F32)
        hg_o[pl.ds(pl.multiple_of(v * WS, 16), WS), :] = out[32:256].astype(BF16)
        sums = jnp.sum(out * SP[v].astype(F32), axis=1, keepdims=True)
        for h in range(2):
            GI[c, pl.ds(2 * v + h, 1)] = as_row(sums[h * 128 : h * 128 + 128])
        return 0

    GI[c, 32:40] = jnp.zeros((8, 128), F32)
    for blk in range(4):
        GI[c, 32 + blk : 33 + blk] = as_row(LAB[blk * 128 : blk * 128 + 128, :])
    lax.fori_loop(0, 8, head_grad, 0)
    r2 = {}
    for k in range(2):
        b = x if k == 0 else y
        at_b = at_x if k == 0 else at_y
        recv(r1[k][0], RH.at[k, 0])
        for o_ in range(2):
            R[k, m4(b + 1), o_] = (R[k, m4(b + 1), o_].astype(F32) + RH[k, 0, o_].astype(F32)).astype(BF16)
        n0 = send(R.at[k, m4(b + 1)], RB.at[k, 0], at_b(1))
        recv(r1[k][1], RH.at[k, 1])
        for o_ in range(2):
            R[k, m4(b - 1), 2 + o_] = (R[k, m4(b - 1), 2 + o_].astype(F32) + RH[k, 1, o_].astype(F32)).astype(BF16)
        n1 = send(R.at[k, m4(b - 1)], RB.at[k, 1], at_b(-1))
        r2[k] = (n0, n1)
    lax.fori_loop(8, 16, head_grad, 0)
    gi = send(GI.at[c], GI.at[c], partner)
    recv(gi, GI.at[pc])
    for x_ in range(4):
        GX[x_, 0:8] = GI[0, 8 * x_ : 8 * x_ + 8] + GI[1, 8 * x_ : 8 * x_ + 8]
        GX[x_, 8:16] = GI[0, 32:40] + GI[1, 32:40]
    GXR[x] = GX[x]
    gx = [send(GX.at[m4(x + d)], GXR.at[x], at_x(d)) for d in (1, 2, 3)]
    r3 = {}
    for k in range(2):
        b, o = (x, y) if k == 0 else (y, x)
        at_o = at_y if k == 0 else at_x
        recv(r2[k][0], RB.at[k, 0])
        recv(r2[k][1], RB.at[k, 1])
        for o_ in range(4):
            Q[k, o_] = (R[k, b, o_].astype(F32) + RB[k, 0, o_].astype(F32) + RB[k, 1, o_].astype(F32)).astype(BF16)
        r3[k] = [send(Q.at[k, m4(o + d)], QR.at[k, d - 1], at_o(d)) for d in (1, 2, 3)]
    for d in (1, 2, 3):
        recv(gx[d - 1], GXR.at[m4(x - d)])
    GY[y] = GXR[0] + GXR[1] + GXR[2] + GXR[3]
    gy = [send(GY.at[y], GY.at[y], at_y(d)) for d in (1, 2, 3)]
    r4 = {}
    for k in range(2):
        o = y if k == 0 else x
        for d in (1, 2, 3):
            recv(r3[k][d - 1], QR.at[k, d - 1])
        W[k] = (Q[k, o].astype(F32) + QR[k, 0].astype(F32) + QR[k, 1].astype(F32) + QR[k, 2].astype(F32)).astype(BF16)
        r4[k] = [send(W.at[k, zidx(m8(z + d))], ZR.at[k, d - 1], at_z(d)) for d in range(1, 8)]
    for d in (1, 2, 3):
        recv(gy[d - 1], GY.at[m4(y - d)])
    GZ[zz] = GY[0] + GY[1] + GY[2] + GY[3]
    gz = [send(GZ.at[zz], GZ.at[zz], at_z(d)) for d in range(1, 8)]
    for k in range(2):
        for d in range(1, 8):
            recv(r4[k][d - 1], ZR.at[k, d - 1])
        got = W[k, zz].astype(F32)
        for d in range(7):
            got = got + ZR[k, d].astype(F32)
        NG[:, k * 128 : k * 128 + 128] = got

    own = pl.ds(pl.multiple_of(dp * 32, 32), 32)
    inv = INVS[own, 0:1]
    ng = NG[...]
    rows = AS[0:32, :]
    gain = AS[32:33, :]
    scaled = ng * gain
    for d in range(1, 8):
        recv(gz[d - 1], GZ.at[zidx(m8(z - d))])
    total = GZ[0]
    for i in range(1, 8):
        total = total + GZ[i]
    GT[...] = total
    wide = jnp.broadcast_to(GT[pl.ds(8 + y, 1)], (32, 128))
    inner = jnp.sum(jnp.where(lane == sub + zh * 32, wide, 0.0), axis=1, keepdims=True) / DS
    out = inv * scaled - rows * (inv * inv) * inner
    rows_o[...] = pltpu.roll(out, 224, 1)[:, 0:WS]
    at = (zl * 2 + c) * 2
    sums = jnp.concatenate([GT[pl.ds(at, 1)], GT[pl.ds(at + 1, 1)]], axis=1)
    sums = sums / jnp.where(lane_iota((1, 256)) < 32, 1.0, gain)
    gain_o[...] = pltpu.roll(jnp.broadcast_to(sums, (8, 256)), 224, 1)[0:1, 0:WS]
    for cp in sent:
        cp.wait_send()


def local(teacher_rows, student_rows, teacher_gain, student_gain, teacher_head, student_head, labels):
    vmem = pl.BlockSpec(memory_space=pltpu.VMEM)
    anyw = pl.BlockSpec(memory_space=pl.ANY)
    V = pltpu.VMEM
    loss, gain_grad, rows_grad, head_grad = pl.pallas_call(
        kernel,
        out_shape=(
            jax.ShapeDtypeStruct((1, 1), F32),
            jax.ShapeDtypeStruct((1, WS), F32),
            jax.ShapeDtypeStruct((32, WS), F32),
            jax.ShapeDtypeStruct((DS, 512), BF16),
        ),
        in_specs=[vmem, vmem, vmem, vmem, vmem, anyw, anyw],
        out_specs=(vmem, vmem, vmem, vmem),
        scratch_shapes=[
            V((4, 4, 2, 4, 8, 32, 128), BF16),
            V((16, 256, 512), BF16),
            V((16, 128, 512), BF16),
            V((16, 256, 512), BF16),
            V((512, 4096), BF16),
            V((512, 512), F32), V((512, 512), F32), V((512, 512), F32),
            V((4, 512, 256), BF16), V((16, 512, 256), BF16),
            V((512, 512), BF16),
            V((512, 512), F32),
            V((40, 384), F32), V((40, 256), F32),
            V((512, 128), F32), V((512, 128), F32), V((512, 128), F32), V((512, 128), F32),
            V((128, 128), F32),
            V((8, 8, 128), F32), V((2, 16, 128), F32), V((4, 24, 128), F32), V((4, 8, 128), F32),
            V((2, 16, 128), F32), V((4, 16, 128), F32), V((4, 16, 128), F32), V((8, 16, 128), F32),
            V((2, 4, 4, 8, 32, 128), BF16), V((2, 4, 4, 8, 32, 128), BF16), V((2, 4, 4, 8, 32, 128), BF16),
            V((2, 2, 2, 8, 32, 128), BF16), V((2, 2, 4, 8, 32, 128), BF16),
            V((2, 4, 8, 32, 128), BF16), V((2, 3, 8, 32, 128), BF16),
            V((2, 8, 32, 128), BF16), V((2, 7, 32, 128), BF16),
            V((32, 256), F32),
            V((2, 40, 128), F32), V((4, 16, 128), F32), V((4, 16, 128), F32),
            V((4, 16, 128), F32), V((8, 16, 128), F32), V((16, 128), F32),
            pltpu.SemaphoreType.DMA((3, 16)),
            pltpu.SemaphoreType.DMA((NSEM,)),
            pltpu.SemaphoreType.DMA((NSEM,)),
        ],
        compiler_params=pltpu.CompilerParams(
            collective_id=0, has_side_effects=True, vmem_limit_bytes=47 << 20
        ),
    )(
        teacher_rows, student_rows, teacher_gain, student_gain,
        labels.reshape(4, 128), teacher_head, student_head,
    )
    return loss.reshape(()), head_grad, gain_grad.reshape(WS), rows_grad


def solution(mesh):
    in_specs = (
        P("dp", "vocab"),
        P("dp", "vocab"),
        P("vocab"),
        P("vocab"),
        P(None, ("dp", "vocab")),
        P(None, ("dp", "vocab")),
        P(),
    )
    out_specs = (P(), P(None, ("dp", "vocab")), P("vocab"), P("dp", "vocab"))
    return jax.shard_map(local, mesh=mesh, in_specs=in_specs, out_specs=out_specs, check_vma=False)
```

```python
import functools

import jax
import jax.numpy as jnp
from jax import lax
from jax.experimental import pallas as pl
from jax.experimental.pallas import tpu as pltpu
from jax.sharding import PartitionSpec as P

MESH = pl.DeviceIdType.MESH
F32 = jnp.float32
BF16 = jnp.bfloat16
DT = 4608
DS = 3584
TOKENS = 512
CAP = 30.0
SCALE = 4096.0
EPS = 1e-06
WT = 288
WS = 224
NSEM = 160


def row_iota(shape):
    return lax.broadcasted_iota(jnp.int32, shape, 0)


def lane_iota(shape):
    return lax.broadcasted_iota(jnp.int32, shape, 1)


def kernel(
    tr_h, sr_h, tg_h, sg_h, lab_h, th, sh,
    loss_o, gain_o, rows_o, hg_o,
    G, TA, TB, SP, SPT, accT, accS, accA, NT, NS, gl, accZ,
    AT, AS, INVT, INVS, ST, LAB, SQ,
    MZ, MC, MX, MY, TC, TX, TY, TZ,
    PS, PR, R, RH, RB, Q, QR, W, ZR, NG,
    GI, GX, GXR, GY, GZ, GT,
    tr, sr, tg, sg, lab, isem, hsem, ssem, rsem,
):
    dp = lax.axis_index("dp")
    vo = lax.axis_index("vocab")
    y, zh = dp // 4, dp % 4
    x, zl, c = vo // 4, (vo // 2) % 2, vo % 2
    z = zh * 2 + zl
    zz = zl * 4 + zh
    pc = 1 - c

    def dev(x_, y_, z_, c_):
        return (y_ * 4 + z_ // 2, x_ * 4 + (z_ % 2) * 2 + c_)

    def m4(v):
        return lax.rem(v + 8, 4)

    def m8(v):
        return lax.rem(v + 16, 8)

    def at_x(d):
        return dev(m4(x + d), y, z, c)

    def at_y(d):
        return dev(x, m4(y + d), z, c)

    def at_z(d):
        return dev(x, y, m8(z + d), c)

    partner = dev(x, y, z, pc)

    def zidx(z_):
        return (z_ % 2) * 4 + z_ // 2

    count = [0]
    sent = []

    def send(src, dst, device):
        n = count[0]
        count[0] += 1
        cp = pltpu.make_async_remote_copy(
            src_ref=src, dst_ref=dst, send_sem=ssem.at[n], recv_sem=rsem.at[n],
            device_id=device, device_id_type=MESH,
        )
        cp.start()
        sent.append(cp)
        return n

    def recv(n, landing):
        pltpu.make_async_remote_copy(
            src_ref=landing, dst_ref=landing, send_sem=ssem.at[n], recv_sem=rsem.at[n],
            device_id=partner, device_id_type=MESH,
        ).wait_recv()

    def head_copies(v):
        v = jnp.int32(v)
        return (
            pltpu.make_async_copy(th.at[pl.ds(pl.multiple_of(v * WT, 16), 256)], TA.at[v], hsem.at[0, v]),
            pltpu.make_async_copy(th.at[pl.ds(pl.multiple_of(v * WT + 256, 16), 32)], TB.at[v, pl.ds(0, 32)], hsem.at[1, v]),
            pltpu.make_async_copy(sh.at[pl.ds(pl.multiple_of(v * WS, 16), WS)], SP.at[v, pl.ds(32, WS)], hsem.at[2, v]),
        )

    def wait_heads(v, _):
        for cp in head_copies(v):
            cp.wait()
        return 0

    own_copies = [
        pltpu.make_async_copy(src, dst, isem.at[i])
        for i, (src, dst) in enumerate(((tr_h, tr), (sr_h, sr), (tg_h, tg), (sg_h, sg), (lab_h, lab)))
    ]
    for cp in own_copies:
        cp.start()
    barrier = pltpu.get_barrier_semaphore()
    others = [partner] + [at_x(d) for d in (1, 2, 3)] + [at_y(d) for d in (1, 2, 3)] + [at_z(d) for d in range(1, 8)]
    for d in others:
        pl.semaphore_signal(barrier, inc=1, device_id=d, device_id_type=MESH)

    AT[...] = jnp.zeros_like(AT)
    AS[...] = jnp.zeros_like(AS)
    for cp in own_copies:
        cp.wait()
    AT[0:32, 0:WT] = tr[...].astype(F32)
    AS[0:32, 0:WS] = sr[...].astype(F32)
    AT[32:40, 0:WT] = jnp.broadcast_to(tg[...].astype(F32).reshape(1, WT), (8, WT))
    AS[32:40, 0:WS] = jnp.broadcast_to(sg[...].astype(F32).reshape(1, WS), (8, WS))
    a_t = AT[...]
    a_s = pltpu.roll(AS[...], 32, 1)
    AS[...] = a_s
    tiles = [a_t[:, 0:128], a_t[:, 128:256], a_t[:, 256:384] + a_s[:, 0:128], a_s[:, 128:256]]
    for j in range(4):
        b, o = (x, y) if j < 2 else (y, x)
        G[j, b, c, o, zz] = tiles[j][0:32].astype(BF16)
    sq_t = jnp.sum(a_t[0:32] * a_t[0:32], axis=1, keepdims=True)
    sq_s = jnp.sum(a_s[0:32] * a_s[0:32], axis=1, keepdims=True)
    sub, lane = row_iota((32, 128)), lane_iota((32, 128))
    MZ[zz] = jnp.zeros((8, 128), F32)
    MZ[zz, 0:1] = jnp.sum(jnp.where(lane == sub, sq_t, 0.0) + jnp.where(lane == sub + 32, sq_s, 0.0), axis=0, keepdims=True)
    for j in range(4):
        MZ[zz, 4 + j : 5 + j] = tiles[j][32:33]

    pl.semaphore_wait(barrier, len(others))

    mz = [send(MZ.at[zz], MZ.at[zz], at_z(d)) for d in range(1, 8)]
    zs = {}

    def z_send(j):
        b, o = (x, y) if j < 2 else (y, x)
        piece = G.at[j, b, c, o, zz]
        zs[j] = [send(piece, piece, at_z(d)) for d in range(1, 8)]

    z_send(0)
    z_send(2)

    def start_heads(v, _):
        for cp in head_copies(v):
            cp.start()
        return 0

    lax.fori_loop(0, 16, start_heads, 0)
    TB[:, 32:128, :] = jnp.zeros((16, 96, 512), BF16)
    SP[:, 0:32, :] = jnp.zeros((16, 32, 512), BF16)
    accT[...] = jnp.zeros_like(accT)
    accS[...] = jnp.zeros_like(accS)

    def axes(j):
        return (x, y, at_x, at_y) if j < 2 else (y, x, at_y, at_x)

    o1, o2, b1, b2, ds = {}, {}, {}, {}, {}

    def z_done(j):
        b, o, at_b, at_o = axes(j)
        for d in range(1, 8):
            recv(zs[j][d - 1], G.at[j, b, c, o, zidx(m8(z - d))])
        block = G.at[j, b, c, o]
        if j in (0, 2):
            o1[j] = [send(block, block, at_o(d)) for d in (1, 2, 3)]
        else:
            o1[j] = [send(block, block, at_o(1)), send(block, block, at_o(-1))]

    def o_near(j):
        b, o, at_b, at_o = axes(j)
        recv(o1[j][0], G.at[j, b, c, m4(o - 1)])
        half = G.at[j, b, c, m4(o - 1), pl.ds(0, 4)]
        f0 = send(half, half, at_o(1))
        recv(o1[j][1], G.at[j, b, c, m4(o + 1)])
        half = G.at[j, b, c, m4(o + 1), pl.ds(4, 4)]
        o2[j] = [f0, send(half, half, at_o(-1))]

    def o_far(j):
        b, o, at_b, at_o = axes(j)
        if j in (0, 2):
            for d in (1, 2, 3):
                recv(o1[j][d - 1], G.at[j, b, c, m4(o - d)])
        else:
            recv(o2[j][0], G.at[j, b, c, m4(o + 2), pl.ds(0, 4)])
            recv(o2[j][1], G.at[j, b, c, m4(o + 2), pl.ds(4, 4)])
        block = G.at[j, b, c]
        b1[j] = [send(block, block, at_b(1)), send(block, block, at_b(-1))]
        ds[j] = [send(block, block, partner)]

    def b_near(j):
        b, o, at_b, at_o = axes(j)
        recv(b1[j][0], G.at[j, m4(b - 1), c])
        half = G.at[j, m4(b - 1), c, pl.ds(0, 2)]
        f0 = send(half, half, at_b(1))
        recv(b1[j][1], G.at[j, m4(b + 1), c])
        half = G.at[j, m4(b + 1), c, pl.ds(2, 2)]
        b2[j] = [f0, send(half, half, at_b(-1))]
        for e in (-1, 1):
            block = G.at[j, m4(b + e), c]
            ds[j].append(send(block, block, partner))

    def b_far(j):
        b, o, at_b, at_o = axes(j)
        far = m4(b + 2)
        recv(b2[j][0], G.at[j, far, c, pl.ds(0, 2)])
        recv(b2[j][1], G.at[j, far, c, pl.ds(2, 2)])
        ds[j].append(send(G.at[j, far, c], G.at[j, far, c], partner))

    def core_done(j, ks):
        b = x if j < 2 else y
        for k in ks:
            recv(ds[j][k], G.at[j, m4(b + (0, -1, 1, 2)[k]), pc])

    z_done(0)
    z_done(2)
    z_send(1)
    z_send(3)
    for d in range(1, 8):
        recv(mz[d - 1], MZ.at[zidx(m8(z - d))])
    MC[c] = jnp.zeros((16, 128), F32)
    for h in range(4):
        MC[c, h : h + 1] = MZ[h, 0:1] + MZ[4 + h, 0:1]
    MC[c, 8:12] = MZ[zh, 4:8]
    MC[c, 12:16] = MZ[4 + zh, 4:8]
    mc = send(MC.at[c], MC.at[c], partner)
    recv(mc, MC.at[pc])
    MX[x] = jnp.zeros((24, 128), F32)
    MX[x, 0:8] = MC[0, 0:8] + MC[1, 0:8]
    MX[x, 8:16] = MC[0, 8:16]
    MX[x, 16:24] = MC[1, 8:16]
    mx = [send(MX.at[x], MX.at[x], at_x(d)) for d in (1, 2, 3)]
    o_far(0)
    o_far(2)
    z_done(1)
    z_done(3)
    for d in (1, 2, 3):
        recv(mx[d - 1], MX.at[m4(x - d)])
    MY[y] = MX[0, 0:8] + MX[1, 0:8] + MX[2, 0:8] + MX[3, 0:8]
    my = [send(MY.at[y], MY.at[y], at_y(d)) for d in (1, 2, 3)]
    o_near(1)
    o_near(3)
    o_far(1)
    o_far(3)
    for d in (1, 2, 3):
        recv(my[d - 1], MY.at[m4(y - d)])
    lane1 = lane_iota((8, 128))
    for yy in range(4):
        sums = MY[yy]
        inv = lax.rsqrt(jnp.where(lane1 < 32, sums / DT, sums / DS) + EPS)
        for h in range(4):
            wide = jnp.broadcast_to(inv[h : h + 1], (32, 128))
            base = (yy * 4 + h) * 32
            INVT[base : base + 32, :] = jnp.broadcast_to(jnp.sum(jnp.where(lane == sub, wide, 0.0), axis=1, keepdims=True), (32, 128))
            INVS[base : base + 32, :] = jnp.broadcast_to(jnp.sum(jnp.where(lane == sub + 32, wide, 0.0), axis=1, keepdims=True), (32, 128))
    sub2, lane2 = row_iota((128, 128)), lane_iota((128, 128))
    for blk in range(4):
        wide = jnp.broadcast_to(lab[blk : blk + 1, :].astype(F32), (128, 128))
        LAB[blk * 128 : blk * 128 + 128, :] = jnp.broadcast_to(jnp.sum(jnp.where(lane2 == sub2, wide, 0.0), axis=1, keepdims=True), (128, 128))
    lax.fori_loop(0, 16, wait_heads, 0)

    def teacher_block(x_):
        def norm(u, _):
            zl_, c_ = u // 2, u % 2
            for j in range(2):
                gain = MX[x_, pl.ds(8 + c_ * 8 + zl_ * 4 + j, 1)]
                for o_ in range(4):
                    rows = G[j, x_, c_, o_, pl.ds(zl_ * 4, 4)].reshape(128, 128).astype(F32)
                    r = rows * INVT[o_ * 128 : o_ * 128 + 128, :] * gain
                    NT[u, o_ * 128 : o_ * 128 + 128, j * 128 : j * 128 + 128] = r.astype(BF16)
            return 0

        lax.fori_loop(0, 4, norm, 0)

        def mul(n, _):
            cols = pl.ds(pl.multiple_of(n * 256, 256), 256)
            lt = jnp.concatenate([NT[u] for u in range(4)], axis=1)
            rt = jnp.concatenate([TA[x_ * 4 + u, :, cols] for u in range(4)], axis=0)
            accT[:, cols] += jnp.dot(lt, rt, preferred_element_type=F32)
            return 0

        lax.fori_loop(0, 2, mul, 0)

    def student_norm(y_):
        tok = pl.ds(pl.multiple_of(y_ * 128, 128), 128)

        def norm(v, _):
            x_, zl_, c_ = v // 4, (v // 2) % 2, v % 2
            for j in range(2):
                gain = MX[x_, pl.ds(8 + c_ * 8 + zl_ * 4 + 2 + j, 1)]
                rows = G[2 + j, y_, c_, x_, pl.ds(zl_ * 4, 4)].reshape(128, 128).astype(F32)
                inv = INVS[tok, :]
                if j == 0:
                    inv = jnp.where(lane2 < 32, INVT[tok, :], inv)
                NS[v, tok, j * 128 : j * 128 + 128] = (rows * inv * gain).astype(BF16)
            return 0

        lax.fori_loop(0, 16, norm, 0)

    def student_block(ys):
        toks = [pl.ds(pl.multiple_of(y_ * 128, 128), 128) for y_ in ys]

        def lhs(q, width):
            return jnp.concatenate(
                [jnp.concatenate([NS[q * 4 + u, tok, 0:width] for u in range(4)], axis=1) for tok in toks], axis=0
            )

        def mul(q, _):
            rs = jnp.concatenate([SP[q * 4 + u] for u in range(4)], axis=0)
            rb = jnp.concatenate([TB[q * 4 + u] for u in range(4)], axis=0)
            s_part = jnp.dot(lhs(q, 256), rs, preferred_element_type=F32)
            t_part = jnp.dot(lhs(q, 128), rb, preferred_element_type=F32)
            for i, tok in enumerate(toks):
                accS[tok, :] += s_part[i * 128 : i * 128 + 128]
                accT[tok, :] += t_part[i * 128 : i * 128 + 128]
            return 0

        lax.fori_loop(0, 4, mul, 0)

    def flip(v, _):
        SPT[:, pl.ds(pl.multiple_of(v * 256, 256), 256)] = jnp.transpose(SP[v])
        return 0

    for j in range(4):
        core_done(j, (0,))
    teacher_block(x)
    student_norm(y)
    b_near(0)
    b_near(2)
    student_block([y])
    b_near(1)
    b_near(3)
    lax.fori_loop(0, 16, flip, 0)
    for j in (0, 1):
        core_done(j, (1, 2))

    def teacher_near(i, _):
        teacher_block(m4(x - 1 + 2 * i))
        return 0

    def student_near(i, _):
        student_norm(m4(y - 1 + 2 * i))
        return 0

    lax.fori_loop(0, 2, teacher_near, 0)
    b_far(0)
    b_far(2)
    for j in (2, 3):
        core_done(j, (1, 2))
    lax.fori_loop(0, 2, student_near, 0)
    b_far(1)
    b_far(3)
    student_block([m4(y - 1), m4(y + 1)])
    for j in range(4):
        core_done(j, (3,))
    teacher_block(m4(x + 2))
    student_norm(m4(y + 2))
    student_block([m4(y + 2)])

    first = (dp * 16 + vo) * 512

    def stats(i, _):
        rows = pl.ds(pl.multiple_of(i * 64, 64), 64)
        tl = CAP * jnp.tanh(accT[rows, :] / CAP)
        sl = CAP * jnp.tanh(accS[rows, :] / CAP)
        et, es = jnp.exp(tl), jnp.exp(sl)
        want = LAB[rows, 0:1]
        hit = (lane_iota((64, 512)) + first).astype(F32) == want
        picked = jnp.sum(jnp.where(hit, sl, 0.0), axis=1, keepdims=True)
        cross = jnp.sum(et * (tl - sl), axis=1, keepdims=True)
        tot_t = jnp.sum(et, axis=1, keepdims=True)
        tot_s = jnp.sum(es, axis=1, keepdims=True)
        ln = lane_iota((64, 128))
        ST[rows, :] = jnp.where(ln == 0, tot_t, jnp.where(ln == 1, tot_s, jnp.where(ln == 2, cross, jnp.where(ln == 3, picked, 0.0))))
        accZ[rows, :] = accS[rows, :]
        slope = SCALE * (1.0 - (sl / CAP) ** 2)
        accA[rows, :] = 1.5 * es * slope
        accT[rows, :] = et * slope
        accS[rows, :] = jnp.where(hit, 0.5 * slope, 0.0)
        return 0

    lax.fori_loop(0, 8, stats, 0)
    for blk in range(4):
        t = jnp.transpose(ST[blk * 128 : blk * 128 + 128, :])
        for q in range(4):
            TC[c, q * 4 + blk : q * 4 + blk + 1] = t[q : q + 1]
    n = send(TC.at[c], TC.at[c], partner)
    recv(n, TC.at[pc])
    TX[x] = TC[0] + TC[1]
    ns = [send(TX.at[x], TX.at[x], at_x(d)) for d in (1, 2, 3)]
    for d in (1, 2, 3):
        recv(ns[d - 1], TX.at[m4(x - d)])
    TY[y] = TX[0] + TX[1] + TX[2] + TX[3]
    ns = [send(TY.at[y], TY.at[y], at_y(d)) for d in (1, 2, 3)]
    for d in (1, 2, 3):
        recv(ns[d - 1], TY.at[m4(y - d)])
    TZ[zz] = TY[0] + TY[1] + TY[2] + TY[3]
    ns = [send(TZ.at[zz], TZ.at[zz], at_z(d)) for d in range(1, 8)]
    for d in range(1, 8):
        recv(ns[d - 1], TZ.at[zidx(m8(z - d))])
    total = TZ[0]
    for i in range(1, 8):
        total = total + TZ[i]
    tt, ts, cr, pk = total[0:4], total[4:8], total[8:12], total[12:16]
    ls = jnp.log(ts)
    token_loss = cr / tt - jnp.log(tt) + ls + 0.5 * (ls - pk)
    loss_o[...] = jnp.sum(jnp.sum(token_loss, axis=1, keepdims=True), axis=0, keepdims=True) / TOKENS
    rec = 1.0 / total[0:8]
    SQ[...] = jnp.zeros_like(SQ)
    for blk in range(4):
        SQ[0:1, :] = rec[blk : blk + 1]
        SQ[1:2, :] = rec[4 + blk : 5 + blk]
        ST[blk * 128 : blk * 128 + 128, :] = jnp.transpose(SQ[...])

    def grads(i, _):
        rows = pl.ds(pl.multiple_of(i * 64, 64), 64)
        g = (accA[rows, :] * ST[rows, 1:2] - accT[rows, :] * ST[rows, 0:1] - accS[rows, :]).astype(BF16)
        gl[rows, :] = g
        dots = jnp.sum(g.astype(F32) * accZ[rows, :], axis=1, keepdims=True)
        LAB[rows, :] = jnp.broadcast_to(dots, (64, 128))
        return 0

    lax.fori_loop(0, 8, grads, 0)

    def as_row(column):
        return jnp.sum(jnp.where(lane2 == sub2, column, 0.0), axis=0, keepdims=True)

    def partial(v):
        return jnp.dot(gl[...], SPT[:, pl.ds(pl.multiple_of(v * 256, 256), 256)], preferred_element_type=F32).astype(BF16)

    def share(dst, x_, c_):
        def one(zl_, _):
            out = partial(x_ * 4 + zl_ * 2 + c_)
            for y_ in range(4):
                part = out[y_ * 128 : y_ * 128 + 128]
                dst[0, x_, y_, pl.ds(zl_ * 4, 4)] = part[:, 0:128].reshape(4, 32, 128)
                dst[1, y_, x_, pl.ds(zl_ * 4, 4)] = part[:, 128:256].reshape(4, 32, 128)
            return 0

        lax.fori_loop(0, 2, one, 0)

    order = [m4(x + 2), m4(x + 1), m4(x - 1), x]
    ps = []
    for x_ in order:
        share(PS, x_, pc)
        ps.append((send(PS.at[0, x_], PR.at[0, x_], partner), send(PS.at[1, :, x_], PR.at[1, :, x_], partner)))
    r1 = {}
    for i, x_ in enumerate(order):
        share(R, x_, c)
        recv(ps[i][0], PR.at[0, x_])
        for o_ in range(4):
            R[0, x_, o_] = (R[0, x_, o_].astype(F32) + PR[0, x_, o_].astype(F32)).astype(BF16)
        recv(ps[i][1], PR.at[1, :, x_])
        for b_ in range(4):
            R[1, b_, x_] = (R[1, b_, x_].astype(F32) + PR[1, b_, x_].astype(F32)).astype(BF16)
        if i == 0:
            r1[0] = (
                send(R.at[0, x_, pl.ds(0, 2)], RH.at[0, 0], at_x(1)),
                send(R.at[0, x_, pl.ds(2, 2)], RH.at[0, 1], at_x(-1)),
            )
    far = m4(y + 2)
    r1[1] = (
        send(R.at[1, far, pl.ds(0, 2)], RH.at[1, 0], at_y(1)),
        send(R.at[1, far, pl.ds(2, 2)], RH.at[1, 1], at_y(-1)),
    )

    def head_grad(v, _):
        out = lax.dot_general(NS[v], gl[...], (((0,), (0,)), ((), ())), preferred_element_type=F32)
        hg_o[pl.ds(pl.multiple_of(v * WS, 16), WS), :] = out[32:256].astype(BF16)
        sums = jnp.sum(out * SP[v].astype(F32), axis=1, keepdims=True)
        for h in range(2):
            GI[c, pl.ds(2 * v + h, 1)] = as_row(sums[h * 128 : h * 128 + 128])
        return 0

    GI[c, 32:40] = jnp.zeros((8, 128), F32)
    for blk in range(4):
        GI[c, 32 + blk : 33 + blk] = as_row(LAB[blk * 128 : blk * 128 + 128, :])
    lax.fori_loop(0, 8, head_grad, 0)
    r2 = {}
    for k in range(2):
        b = x if k == 0 else y
        at_b = at_x if k == 0 else at_y
        recv(r1[k][0], RH.at[k, 0])
        for o_ in range(2):
            R[k, m4(b + 1), o_] = (R[k, m4(b + 1), o_].astype(F32) + RH[k, 0, o_].astype(F32)).astype(BF16)
        n0 = send(R.at[k, m4(b + 1)], RB.at[k, 0], at_b(1))
        recv(r1[k][1], RH.at[k, 1])
        for o_ in range(2):
            R[k, m4(b - 1), 2 + o_] = (R[k, m4(b - 1), 2 + o_].astype(F32) + RH[k, 1, o_].astype(F32)).astype(BF16)
        n1 = send(R.at[k, m4(b - 1)], RB.at[k, 1], at_b(-1))
        r2[k] = (n0, n1)
    lax.fori_loop(8, 16, head_grad, 0)
    gi = send(GI.at[c], GI.at[c], partner)
    recv(gi, GI.at[pc])
    for x_ in range(4):
        GX[x_, 0:8] = GI[0, 8 * x_ : 8 * x_ + 8] + GI[1, 8 * x_ : 8 * x_ + 8]
        GX[x_, 8:16] = GI[0, 32:40] + GI[1, 32:40]
    GXR[x] = GX[x]
    gx = [send(GX.at[m4(x + d)], GXR.at[x], at_x(d)) for d in (1, 2, 3)]
    r3 = {}
    for k in range(2):
        b, o = (x, y) if k == 0 else (y, x)
        at_o = at_y if k == 0 else at_x
        recv(r2[k][0], RB.at[k, 0])
        recv(r2[k][1], RB.at[k, 1])
        for o_ in range(4):
            Q[k, o_] = (R[k, b, o_].astype(F32) + RB[k, 0, o_].astype(F32) + RB[k, 1, o_].astype(F32)).astype(BF16)
        r3[k] = [send(Q.at[k, m4(o + d)], QR.at[k, d - 1], at_o(d)) for d in (1, 2, 3)]
    for d in (1, 2, 3):
        recv(gx[d - 1], GXR.at[m4(x - d)])
    GY[y] = GXR[0] + GXR[1] + GXR[2] + GXR[3]
    gy = [send(GY.at[y], GY.at[y], at_y(d)) for d in (1, 2, 3)]
    r4 = {}
    for k in range(2):
        o = y if k == 0 else x
        for d in (1, 2, 3):
            recv(r3[k][d - 1], QR.at[k, d - 1])
        W[k] = (Q[k, o].astype(F32) + QR[k, 0].astype(F32) + QR[k, 1].astype(F32) + QR[k, 2].astype(F32)).astype(BF16)
        r4[k] = [send(W.at[k, zidx(m8(z + d))], ZR.at[k, d - 1], at_z(d)) for d in range(1, 8)]
    for d in (1, 2, 3):
        recv(gy[d - 1], GY.at[m4(y - d)])
    GZ[zz] = GY[0] + GY[1] + GY[2] + GY[3]
    gz = [send(GZ.at[zz], GZ.at[zz], at_z(d)) for d in range(1, 8)]
    for k in range(2):
        for d in range(1, 8):
            recv(r4[k][d - 1], ZR.at[k, d - 1])
        got = W[k, zz].astype(F32)
        for d in range(7):
            got = got + ZR[k, d].astype(F32)
        NG[:, k * 128 : k * 128 + 128] = got

    own = pl.ds(pl.multiple_of(dp * 32, 32), 32)
    inv = INVS[own, 0:1]
    ng = NG[...]
    rows = AS[0:32, :]
    gain = AS[32:33, :]
    scaled = ng * gain
    for d in range(1, 8):
        recv(gz[d - 1], GZ.at[zidx(m8(z - d))])
    total = GZ[0]
    for i in range(1, 8):
        total = total + GZ[i]
    GT[...] = total
    wide = jnp.broadcast_to(GT[pl.ds(8 + y, 1)], (32, 128))
    inner = jnp.sum(jnp.where(lane == sub + zh * 32, wide, 0.0), axis=1, keepdims=True) / DS
    out = inv * scaled - rows * (inv * inv) * inner
    rows_o[...] = pltpu.roll(out, 224, 1)[:, 0:WS]
    at = (zl * 2 + c) * 2
    sums = jnp.concatenate([GT[pl.ds(at, 1)], GT[pl.ds(at + 1, 1)]], axis=1)
    sums = sums / jnp.where(lane_iota((1, 256)) < 32, 1.0, gain)
    gain_o[...] = pltpu.roll(jnp.broadcast_to(sums, (8, 256)), 224, 1)[0:1, 0:WS]
    for cp in sent:
        cp.wait_send()


def hand_over(gain_i, rows_i, hg_i, gain_o, rows_o, hg_o, sem):
    copies = [pltpu.make_async_copy(gain_i, gain_o, sem.at[4]), pltpu.make_async_copy(rows_i, rows_o, sem.at[5])]
    for i in range(4):
        part = pl.ds(i * 896, 896)
        copies.append(pltpu.make_async_copy(hg_i.at[part], hg_o.at[part], sem.at[i]))
    for cp in copies:
        cp.start()
    for cp in copies:
        cp.wait()


def local(teacher_rows, student_rows, teacher_gain, student_gain, teacher_head, student_head, labels):
    vmem = pl.BlockSpec(memory_space=pltpu.VMEM)
    anyw = pl.BlockSpec(memory_space=pl.ANY)
    hbm = pl.BlockSpec(memory_space=pltpu.HBM)
    V = pltpu.VMEM
    loss, gain_grad, rows_grad, head_grad = pl.pallas_call(
        kernel,
        out_shape=(
            jax.ShapeDtypeStruct((1, 1), F32),
            jax.ShapeDtypeStruct((1, WS), F32),
            jax.ShapeDtypeStruct((32, WS), F32),
            jax.ShapeDtypeStruct((DS, 512), BF16),
        ),
        in_specs=[hbm] * 7,
        out_specs=(vmem, vmem, vmem, vmem),
        scratch_shapes=[
            V((4, 4, 2, 4, 8, 32, 128), BF16),
            V((16, 256, 512), BF16),
            V((16, 128, 512), BF16),
            V((16, 256, 512), BF16),
            V((512, 4096), BF16),
            V((512, 512), F32), V((512, 512), F32), V((512, 512), F32),
            V((4, 512, 256), BF16), V((16, 512, 256), BF16),
            V((512, 512), BF16),
            V((512, 512), F32),
            V((40, 384), F32), V((40, 256), F32),
            V((512, 128), F32), V((512, 128), F32), V((512, 128), F32), V((512, 128), F32),
            V((128, 128), F32),
            V((8, 8, 128), F32), V((2, 16, 128), F32), V((4, 24, 128), F32), V((4, 8, 128), F32),
            V((2, 16, 128), F32), V((4, 16, 128), F32), V((4, 16, 128), F32), V((8, 16, 128), F32),
            V((2, 4, 4, 8, 32, 128), BF16), V((2, 4, 4, 8, 32, 128), BF16), V((2, 4, 4, 8, 32, 128), BF16),
            V((2, 2, 2, 8, 32, 128), BF16), V((2, 2, 4, 8, 32, 128), BF16),
            V((2, 4, 8, 32, 128), BF16), V((2, 3, 8, 32, 128), BF16),
            V((2, 8, 32, 128), BF16), V((2, 7, 32, 128), BF16),
            V((32, 256), F32),
            V((2, 40, 128), F32), V((4, 16, 128), F32), V((4, 16, 128), F32),
            V((4, 16, 128), F32), V((8, 16, 128), F32), V((16, 128), F32),
            V((32, WT), BF16), V((32, WS), BF16), V((WT,), BF16), V((WS,), BF16), V((4, 128), jnp.int32),
            pltpu.SemaphoreType.DMA((5,)),
            pltpu.SemaphoreType.DMA((3, 16)),
            pltpu.SemaphoreType.DMA((NSEM,)),
            pltpu.SemaphoreType.DMA((NSEM,)),
        ],
        compiler_params=pltpu.CompilerParams(
            collective_id=0, has_side_effects=True, vmem_limit_bytes=47 << 20
        ),
    )(
        teacher_rows, student_rows, teacher_gain, student_gain,
        labels.reshape(4, 128), teacher_head, student_head,
    )
    gain_grad, rows_grad, head_grad = pl.pallas_call(
        hand_over,
        out_shape=(
            jax.ShapeDtypeStruct((1, WS), F32),
            jax.ShapeDtypeStruct((32, WS), F32),
            jax.ShapeDtypeStruct((DS, 512), BF16),
        ),
        in_specs=[anyw] * 3,
        out_specs=(hbm, hbm, hbm),
        scratch_shapes=[pltpu.SemaphoreType.DMA((6,))],
        compiler_params=pltpu.CompilerParams(vmem_limit_bytes=8 << 20),
    )(gain_grad, rows_grad, head_grad)
    return loss.reshape(()), head_grad, gain_grad.reshape(WS), rows_grad


def solution(mesh):
    in_specs = (
        P("dp", "vocab"),
        P("dp", "vocab"),
        P("vocab"),
        P("vocab"),
        P(None, ("dp", "vocab")),
        P(None, ("dp", "vocab")),
        P(),
    )
    out_specs = (P(), P(None, ("dp", "vocab")), P("vocab"), P("dp", "vocab"))
    return jax.shard_map(local, mesh=mesh, in_specs=in_specs, out_specs=out_specs, check_vma=False)
```

```python
import functools

import jax
import jax.numpy as jnp
from jax import lax
from jax.experimental import pallas as pl
from jax.experimental.pallas import tpu as pltpu
from jax.sharding import PartitionSpec as P

MESH = pl.DeviceIdType.MESH
F32 = jnp.float32
BF16 = jnp.bfloat16
DT = 4608
DS = 3584
TOKENS = 512
CAP = 30.0
SCALE = 4096.0
EPS = 1e-06
WT = 288
WS = 224
NSEM = 240


def row_iota(shape):
    return lax.broadcasted_iota(jnp.int32, shape, 0)


def lane_iota(shape):
    return lax.broadcasted_iota(jnp.int32, shape, 1)


def kernel(
    tr_h, sr_h, tg_h, sg_h, lab_h, th, sh,
    loss_o, gain_o, rows_o, hg_o,
    G, TA, TB, SP, SPT, accT, accS, accA, NT, NS, gl, accZ,
    AT, AS, INVT, INVS, ST, LAB, SQ,
    MZ, MC, MX, MY, TC, TX, TY, TZ,
    PS, PR, R, RH, RB, Q, QR, W, ZR, NG,
    GI, GX, GXR, GY, GZ, GT,
    tr, sr, tg, sg, lab, isem, hsem, ssem, rsem,
):
    dp = lax.axis_index("dp")
    vo = lax.axis_index("vocab")
    y, zh = dp // 4, dp % 4
    x, zl, c = vo // 4, (vo // 2) % 2, vo % 2
    z = zh * 2 + zl
    zz = zl * 4 + zh
    pc = 1 - c

    def dev(x_, y_, z_, c_):
        return (y_ * 4 + z_ // 2, x_ * 4 + (z_ % 2) * 2 + c_)

    def m4(v):
        return lax.rem(v + 8, 4)

    def m8(v):
        return lax.rem(v + 16, 8)

    def at_x(d):
        return dev(m4(x + d), y, z, c)

    def at_y(d):
        return dev(x, m4(y + d), z, c)

    def at_z(d):
        return dev(x, y, m8(z + d), c)

    partner = dev(x, y, z, pc)

    def zidx(z_):
        return (z_ % 2) * 4 + z_ // 2

    count = [0]
    sent = []

    def send(src, dst, device):
        n = count[0]
        count[0] += 1
        cp = pltpu.make_async_remote_copy(
            src_ref=src, dst_ref=dst, send_sem=ssem.at[n], recv_sem=rsem.at[n],
            device_id=device, device_id_type=MESH,
        )
        cp.start()
        sent.append(cp)
        return n

    def recv(n, landing):
        pltpu.make_async_remote_copy(
            src_ref=landing, dst_ref=landing, send_sem=ssem.at[n], recv_sem=rsem.at[n],
            device_id=partner, device_id_type=MESH,
        ).wait_recv()

    def head_copies(v):
        v = jnp.int32(v)
        return (
            pltpu.make_async_copy(th.at[pl.ds(pl.multiple_of(v * WT, 16), 256)], TA.at[v], hsem.at[0, v]),
            pltpu.make_async_copy(th.at[pl.ds(pl.multiple_of(v * WT + 256, 16), 32)], TB.at[v, pl.ds(0, 32)], hsem.at[1, v]),
            pltpu.make_async_copy(sh.at[pl.ds(pl.multiple_of(v * WS, 16), WS)], SP.at[v, pl.ds(32, WS)], hsem.at[2, v]),
        )

    def wait_heads(v, _):
        for cp in head_copies(v):
            cp.wait()
        return 0

    own_copies = [
        pltpu.make_async_copy(src, dst, isem.at[i])
        for i, (src, dst) in enumerate(((tr_h, tr), (sr_h, sr), (tg_h, tg), (sg_h, sg), (lab_h, lab)))
    ]
    for cp in own_copies:
        cp.start()
    barrier = pltpu.get_barrier_semaphore()
    others = [partner] + [at_x(d) for d in (1, 2, 3)] + [at_y(d) for d in (1, 2, 3)] + [at_z(d) for d in range(1, 8)]
    for d in others:
        pl.semaphore_signal(barrier, inc=1, device_id=d, device_id_type=MESH)

    AT[...] = jnp.zeros_like(AT)
    AS[...] = jnp.zeros_like(AS)
    for cp in own_copies:
        cp.wait()
    AT[0:32, 0:WT] = tr[...].astype(F32)
    AS[0:32, 0:WS] = sr[...].astype(F32)
    AT[32:40, 0:WT] = jnp.broadcast_to(tg[...].astype(F32).reshape(1, WT), (8, WT))
    AS[32:40, 0:WS] = jnp.broadcast_to(sg[...].astype(F32).reshape(1, WS), (8, WS))
    a_t = AT[...]
    a_s = pltpu.roll(AS[...], 32, 1)
    AS[...] = a_s
    tiles = [a_t[:, 0:128], a_t[:, 128:256], a_t[:, 256:384] + a_s[:, 0:128], a_s[:, 128:256]]
    for j in range(4):
        b, o = (x, y) if j < 2 else (y, x)
        G[j, b, c, o, zz] = tiles[j][0:32].astype(BF16)
    sq_t = jnp.sum(a_t[0:32] * a_t[0:32], axis=1, keepdims=True)
    sq_s = jnp.sum(a_s[0:32] * a_s[0:32], axis=1, keepdims=True)
    sub, lane = row_iota((32, 128)), lane_iota((32, 128))
    MZ[zz] = jnp.zeros((8, 128), F32)
    MZ[zz, 0:1] = jnp.sum(jnp.where(lane == sub, sq_t, 0.0) + jnp.where(lane == sub + 32, sq_s, 0.0), axis=0, keepdims=True)
    for j in range(4):
        MZ[zz, 4 + j : 5 + j] = tiles[j][32:33]

    pl.semaphore_wait(barrier, len(others))

    mz = [send(MZ.at[zz], MZ.at[zz], at_z(d)) for d in range(1, 8)]
    zs = {}

    def z_send(j):
        b, o = (x, y) if j < 2 else (y, x)
        piece = G.at[j, b, c, o, zz]
        zs[j] = [send(piece, piece, at_z(d)) for d in range(1, 8)]

    z_send(0)
    z_send(2)

    def start_heads(v, _):
        for cp in head_copies(v):
            cp.start()
        return 0

    lax.fori_loop(0, 16, start_heads, 0)
    TB[:, 32:128, :] = jnp.zeros((16, 96, 512), BF16)
    SP[:, 0:32, :] = jnp.zeros((16, 32, 512), BF16)
    accT[...] = jnp.zeros_like(accT)
    accS[...] = jnp.zeros_like(accS)

    def axes(j):
        return (x, y, at_x, at_y) if j < 2 else (y, x, at_y, at_x)

    o1, o2, b1, b2, ds = {}, {}, {}, {}, {}

    def z_done(j):
        b, o, at_b, at_o = axes(j)
        for d in range(1, 8):
            recv(zs[j][d - 1], G.at[j, b, c, o, zidx(m8(z - d))])
        block = G.at[j, b, c, o]
        if j in (0, 2):
            o1[j] = [send(block, block, at_o(d)) for d in (1, 2, 3)]
        else:
            o1[j] = [send(block, block, at_o(1)), send(block, block, at_o(-1))]

    def o_near(j):
        b, o, at_b, at_o = axes(j)
        recv(o1[j][0], G.at[j, b, c, m4(o - 1)])
        half = G.at[j, b, c, m4(o - 1), pl.ds(0, 4)]
        f0 = send(half, half, at_o(1))
        recv(o1[j][1], G.at[j, b, c, m4(o + 1)])
        half = G.at[j, b, c, m4(o + 1), pl.ds(4, 4)]
        o2[j] = [f0, send(half, half, at_o(-1))]

    def o_far(j):
        b, o, at_b, at_o = axes(j)
        if j in (0, 2):
            for d in (1, 2, 3):
                recv(o1[j][d - 1], G.at[j, b, c, m4(o - d)])
        else:
            recv(o2[j][0], G.at[j, b, c, m4(o + 2), pl.ds(0, 4)])
            recv(o2[j][1], G.at[j, b, c, m4(o + 2), pl.ds(4, 4)])
        block = G.at[j, b, c]
        b1[j] = [send(block, block, at_b(1)), send(block, block, at_b(-1))]
        ds[j] = [send(block, block, partner)]

    def b_near(j):
        b, o, at_b, at_o = axes(j)
        recv(b1[j][0], G.at[j, m4(b - 1), c])
        half = G.at[j, m4(b - 1), c, pl.ds(0, 2)]
        f0 = send(half, half, at_b(1))
        recv(b1[j][1], G.at[j, m4(b + 1), c])
        half = G.at[j, m4(b + 1), c, pl.ds(2, 2)]
        b2[j] = [f0, send(half, half, at_b(-1))]
        for e in (-1, 1):
            block = G.at[j, m4(b + e), c]
            ds[j].append(send(block, block, partner))

    def b_far(j):
        b, o, at_b, at_o = axes(j)
        far = m4(b + 2)
        recv(b2[j][0], G.at[j, far, c, pl.ds(0, 2)])
        recv(b2[j][1], G.at[j, far, c, pl.ds(2, 2)])
        ds[j].append(send(G.at[j, far, c], G.at[j, far, c], partner))

    def core_done(j, ks):
        b = x if j < 2 else y
        for k in ks:
            recv(ds[j][k], G.at[j, m4(b + (0, -1, 1, 2)[k]), pc])

    z_done(0)
    z_done(2)
    z_send(1)
    z_send(3)
    for d in range(1, 8):
        recv(mz[d - 1], MZ.at[zidx(m8(z - d))])
    MC[c] = jnp.zeros((16, 128), F32)
    for h in range(4):
        MC[c, h : h + 1] = MZ[h, 0:1] + MZ[4 + h, 0:1]
    MC[c, 8:12] = MZ[zh, 4:8]
    MC[c, 12:16] = MZ[4 + zh, 4:8]
    mc = send(MC.at[c], MC.at[c], partner)
    recv(mc, MC.at[pc])
    MX[x] = jnp.zeros((24, 128), F32)
    MX[x, 0:8] = MC[0, 0:8] + MC[1, 0:8]
    MX[x, 8:16] = MC[0, 8:16]
    MX[x, 16:24] = MC[1, 8:16]
    mx = [send(MX.at[x], MX.at[x], at_x(d)) for d in (1, 2, 3)]
    o_far(0)
    o_far(2)
    z_done(1)
    z_done(3)
    for d in (1, 2, 3):
        recv(mx[d - 1], MX.at[m4(x - d)])
    MY[y] = MX[0, 0:8] + MX[1, 0:8] + MX[2, 0:8] + MX[3, 0:8]
    my = [send(MY.at[y], MY.at[y], at_y(d)) for d in (1, 2, 3)]
    o_near(1)
    o_near(3)
    o_far(1)
    o_far(3)
    for d in (1, 2, 3):
        recv(my[d - 1], MY.at[m4(y - d)])
    lane1 = lane_iota((8, 128))
    for yy in range(4):
        sums = MY[yy]
        inv = lax.rsqrt(jnp.where(lane1 < 32, sums / DT, sums / DS) + EPS)
        for h in range(4):
            wide = jnp.broadcast_to(inv[h : h + 1], (32, 128))
            base = (yy * 4 + h) * 32
            INVT[base : base + 32, :] = jnp.broadcast_to(jnp.sum(jnp.where(lane == sub, wide, 0.0), axis=1, keepdims=True), (32, 128))
            INVS[base : base + 32, :] = jnp.broadcast_to(jnp.sum(jnp.where(lane == sub + 32, wide, 0.0), axis=1, keepdims=True), (32, 128))
    sub2, lane2 = row_iota((128, 128)), lane_iota((128, 128))
    for blk in range(4):
        wide = jnp.broadcast_to(lab[blk : blk + 1, :].astype(F32), (128, 128))
        LAB[blk * 128 : blk * 128 + 128, :] = jnp.broadcast_to(jnp.sum(jnp.where(lane2 == sub2, wide, 0.0), axis=1, keepdims=True), (128, 128))
    lax.fori_loop(0, 16, wait_heads, 0)

    def teacher_block(x_):
        def norm(u, _):
            zl_, c_ = u // 2, u % 2
            for j in range(2):
                gain = MX[x_, pl.ds(8 + c_ * 8 + zl_ * 4 + j, 1)]
                for o_ in range(4):
                    rows = G[j, x_, c_, o_, pl.ds(zl_ * 4, 4)].reshape(128, 128).astype(F32)
                    r = rows * INVT[o_ * 128 : o_ * 128 + 128, :] * gain
                    NT[u, o_ * 128 : o_ * 128 + 128, j * 128 : j * 128 + 128] = r.astype(BF16)
            return 0

        lax.fori_loop(0, 4, norm, 0)

        def mul(n, _):
            cols = pl.ds(pl.multiple_of(n * 256, 256), 256)
            lt = jnp.concatenate([NT[u] for u in range(4)], axis=1)
            rt = jnp.concatenate([TA[x_ * 4 + u, :, cols] for u in range(4)], axis=0)
            accT[:, cols] += jnp.dot(lt, rt, preferred_element_type=F32)
            return 0

        lax.fori_loop(0, 2, mul, 0)

    def student_norm(y_):
        tok = pl.ds(pl.multiple_of(y_ * 128, 128), 128)

        def norm(v, _):
            x_, zl_, c_ = v // 4, (v // 2) % 2, v % 2
            for j in range(2):
                gain = MX[x_, pl.ds(8 + c_ * 8 + zl_ * 4 + 2 + j, 1)]
                rows = G[2 + j, y_, c_, x_, pl.ds(zl_ * 4, 4)].reshape(128, 128).astype(F32)
                inv = INVS[tok, :]
                if j == 0:
                    inv = jnp.where(lane2 < 32, INVT[tok, :], inv)
                NS[v, tok, j * 128 : j * 128 + 128] = (rows * inv * gain).astype(BF16)
            return 0

        lax.fori_loop(0, 16, norm, 0)

    def student_block(ys):
        toks = [pl.ds(pl.multiple_of(y_ * 128, 128), 128) for y_ in ys]

        def lhs(q, width):
            return jnp.concatenate(
                [jnp.concatenate([NS[q * 4 + u, tok, 0:width] for u in range(4)], axis=1) for tok in toks], axis=0
            )

        def mul(q, _):
            rs = jnp.concatenate([SP[q * 4 + u] for u in range(4)], axis=0)
            rb = jnp.concatenate([TB[q * 4 + u] for u in range(4)], axis=0)
            s_part = jnp.dot(lhs(q, 256), rs, preferred_element_type=F32)
            t_part = jnp.dot(lhs(q, 128), rb, preferred_element_type=F32)
            for i, tok in enumerate(toks):
                accS[tok, :] += s_part[i * 128 : i * 128 + 128]
                accT[tok, :] += t_part[i * 128 : i * 128 + 128]
            return 0

        lax.fori_loop(0, 4, mul, 0)

    def flip(v, _):
        SPT[:, pl.ds(pl.multiple_of(v * 256, 256), 256)] = jnp.transpose(SP[v])
        return 0

    for j in range(4):
        core_done(j, (0,))
    teacher_block(x)
    student_norm(y)
    b_near(0)
    b_near(2)
    student_block([y])
    b_near(1)
    b_near(3)
    lax.fori_loop(0, 16, flip, 0)
    for j in (0, 1):
        core_done(j, (1, 2))

    def teacher_near(i, _):
        teacher_block(m4(x - 1 + 2 * i))
        return 0

    def student_near(i, _):
        student_norm(m4(y - 1 + 2 * i))
        return 0

    lax.fori_loop(0, 2, teacher_near, 0)
    b_far(0)
    b_far(2)
    for j in (2, 3):
        core_done(j, (1, 2))
    lax.fori_loop(0, 2, student_near, 0)
    b_far(1)
    b_far(3)
    student_block([m4(y - 1), m4(y + 1)])
    for j in range(4):
        core_done(j, (3,))
    teacher_block(m4(x + 2))
    student_norm(m4(y + 2))
    student_block([m4(y + 2)])

    first = (dp * 16 + vo) * 512

    def stats(i, _):
        rows = pl.ds(pl.multiple_of(i * 64, 64), 64)
        tl = CAP * jnp.tanh(accT[rows, :] / CAP)
        sl = CAP * jnp.tanh(accS[rows, :] / CAP)
        et, es = jnp.exp(tl), jnp.exp(sl)
        want = LAB[rows, 0:1]
        hit = (lane_iota((64, 512)) + first).astype(F32) == want
        picked = jnp.sum(jnp.where(hit, sl, 0.0), axis=1, keepdims=True)
        cross = jnp.sum(et * (tl - sl), axis=1, keepdims=True)
        tot_t = jnp.sum(et, axis=1, keepdims=True)
        tot_s = jnp.sum(es, axis=1, keepdims=True)
        ln = lane_iota((64, 128))
        ST[rows, :] = jnp.where(ln == 0, tot_t, jnp.where(ln == 1, tot_s, jnp.where(ln == 2, cross, jnp.where(ln == 3, picked, 0.0))))
        accZ[rows, :] = accS[rows, :]
        slope = SCALE * (1.0 - (sl / CAP) ** 2)
        accA[rows, :] = 1.5 * es * slope
        accT[rows, :] = et * slope
        accS[rows, :] = jnp.where(hit, 0.5 * slope, 0.0)
        return 0

    lax.fori_loop(0, 8, stats, 0)
    for blk in range(4):
        t = jnp.transpose(ST[blk * 128 : blk * 128 + 128, :])
        for q in range(4):
            TC[c, q * 4 + blk : q * 4 + blk + 1] = t[q : q + 1]
    n = send(TC.at[c], TC.at[c], partner)
    recv(n, TC.at[pc])
    TX[x] = TC[0] + TC[1]
    ns = [send(TX.at[x], TX.at[x], at_x(d)) for d in (1, 2, 3)]
    for d in (1, 2, 3):
        recv(ns[d - 1], TX.at[m4(x - d)])
    TY[y] = TX[0] + TX[1] + TX[2] + TX[3]
    ns = [send(TY.at[y], TY.at[y], at_y(d)) for d in (1, 2, 3)]
    for d in (1, 2, 3):
        recv(ns[d - 1], TY.at[m4(y - d)])
    TZ[zz] = TY[0] + TY[1] + TY[2] + TY[3]
    ns = [send(TZ.at[zz], TZ.at[zz], at_z(d)) for d in range(1, 8)]
    for d in range(1, 8):
        recv(ns[d - 1], TZ.at[zidx(m8(z - d))])
    total = TZ[0]
    for i in range(1, 8):
        total = total + TZ[i]
    tt, ts, cr, pk = total[0:4], total[4:8], total[8:12], total[12:16]
    ls = jnp.log(ts)
    token_loss = cr / tt - jnp.log(tt) + ls + 0.5 * (ls - pk)
    loss_o[...] = jnp.sum(jnp.sum(token_loss, axis=1, keepdims=True), axis=0, keepdims=True) / TOKENS
    rec = 1.0 / total[0:8]
    SQ[...] = jnp.zeros_like(SQ)
    for blk in range(4):
        SQ[0:1, :] = rec[blk : blk + 1]
        SQ[1:2, :] = rec[4 + blk : 5 + blk]
        ST[blk * 128 : blk * 128 + 128, :] = jnp.transpose(SQ[...])

    def grads(i, _):
        rows = pl.ds(pl.multiple_of(i * 64, 64), 64)
        g = (accA[rows, :] * ST[rows, 1:2] - accT[rows, :] * ST[rows, 0:1] - accS[rows, :]).astype(BF16)
        gl[rows, :] = g
        dots = jnp.sum(g.astype(F32) * accZ[rows, :], axis=1, keepdims=True)
        LAB[rows, :] = jnp.broadcast_to(dots, (64, 128))
        return 0

    lax.fori_loop(0, 8, grads, 0)

    def as_row(column):
        return jnp.sum(jnp.where(lane2 == sub2, column, 0.0), axis=0, keepdims=True)

    def partial(v):
        return jnp.dot(gl[...], SPT[:, pl.ds(pl.multiple_of(v * 256, 256), 256)], preferred_element_type=F32).astype(BF16)

    def share(dst, x_, c_):
        def one(zl_, _):
            out = partial(x_ * 4 + zl_ * 2 + c_)
            for y_ in range(4):
                part = out[y_ * 128 : y_ * 128 + 128]
                dst[0, x_, y_, pl.ds(zl_ * 4, 4)] = part[:, 0:128].reshape(4, 32, 128)
                dst[1, y_, x_, pl.ds(zl_ * 4, 4)] = part[:, 128:256].reshape(4, 32, 128)
            return 0

        lax.fori_loop(0, 2, one, 0)

    order = [m4(x + 2), m4(x + 1), m4(x - 1), x]
    ps = []
    for x_ in order:
        share(PS, x_, pc)
        ps.append((send(PS.at[0, x_], PR.at[0, x_], partner), send(PS.at[1, :, x_], PR.at[1, :, x_], partner)))
    r1 = {}
    row_order = ((2, 0, 0), (-1, 1, 0), (1, 0, 1), (0, 1, 1))

    def far_row(k, e, way, n):
        b, o, at_b = (x, y, at_x) if k == 0 else (y, x, at_y)
        r1[k, e] = send(R.at[k, m4(b + 2), m4(o + e)], RH.at[k, way, n], at_b(1 - 2 * way))

    for i, x_ in enumerate(order):
        share(R, x_, c)
        recv(ps[i][0], PR.at[0, x_])
        for o_ in range(4):
            R[0, x_, o_] = (R[0, x_, o_].astype(F32) + PR[0, x_, o_].astype(F32)).astype(BF16)
        recv(ps[i][1], PR.at[1, :, x_])
        for b_ in range(4):
            R[1, b_, x_] = (R[1, b_, x_].astype(F32) + PR[1, b_, x_].astype(F32)).astype(BF16)
        if i == 0:
            for row in row_order:
                far_row(0, *row)
        far_row(1, *row_order[(0, 2, 1, 3)[i]])

    def head_grad(v, _):
        out = lax.dot_general(NS[v], gl[...], (((0,), (0,)), ((), ())), preferred_element_type=F32)
        hg_o[pl.ds(pl.multiple_of(v * WS, 16), WS), :] = out[32:256].astype(BF16)
        sums = jnp.sum(out * SP[v].astype(F32), axis=1, keepdims=True)
        for h in range(2):
            GI[c, pl.ds(2 * v + h, 1)] = as_row(sums[h * 128 : h * 128 + 128])
        return 0

    GI[c, 32:40] = jnp.zeros((8, 128), F32)
    for blk in range(4):
        GI[c, 32 + blk : 33 + blk] = as_row(LAB[blk * 128 : blk * 128 + 128, :])
    lax.fori_loop(0, 8, head_grad, 0)
    r2 = {}
    for i, (e, way, n) in enumerate(row_order):
        for k in range(2):
            b, o, at_b = (x, y, at_x) if k == 0 else (y, x, at_y)
            r = m4(o + e)
            recv(r1[k, e], RH.at[k, way, n])
            near = m4(b + 1 - 2 * way)
            R[k, near, r] = (R[k, near, r].astype(F32) + RH[k, way, n].astype(F32)).astype(BF16)
            r2[k, e] = (
                send(R.at[k, m4(b + 1), r], RB.at[k, 0, i], at_b(1)),
                send(R.at[k, m4(b - 1), r], RB.at[k, 1, i], at_b(-1)),
            )
    lax.fori_loop(8, 16, head_grad, 0)
    gi = send(GI.at[c], GI.at[c], partner)
    recv(gi, GI.at[pc])
    for x_ in range(4):
        GX[x_, 0:8] = GI[0, 8 * x_ : 8 * x_ + 8] + GI[1, 8 * x_ : 8 * x_ + 8]
        GX[x_, 8:16] = GI[0, 32:40] + GI[1, 32:40]
    GXR[x] = GX[x]
    gx = [send(GX.at[m4(x + d)], GXR.at[x], at_x(d)) for d in (1, 2, 3)]
    r3 = {}
    for i, (e, way, n) in enumerate(row_order):
        for k in range(2):
            b, o, at_o = (x, y, at_y) if k == 0 else (y, x, at_x)
            r = m4(o + e)
            recv(r2[k, e][0], RB.at[k, 0, i])
            recv(r2[k, e][1], RB.at[k, 1, i])
            Q[k, r] = (R[k, b, r].astype(F32) + RB[k, 0, i].astype(F32) + RB[k, 1, i].astype(F32)).astype(BF16)
            if e != 0:
                r3[k, e % 4] = send(Q.at[k, r], QR.at[k, e % 4 - 1], at_o(e))
    for d in (1, 2, 3):
        recv(gx[d - 1], GXR.at[m4(x - d)])
    GY[y] = GXR[0] + GXR[1] + GXR[2] + GXR[3]
    gy = [send(GY.at[y], GY.at[y], at_y(d)) for d in (1, 2, 3)]
    r4 = {}
    for k in range(2):
        o = y if k == 0 else x
        for d in (1, 2, 3):
            recv(r3[k, d], QR.at[k, d - 1])
        W[k] = (Q[k, o].astype(F32) + QR[k, 0].astype(F32) + QR[k, 1].astype(F32) + QR[k, 2].astype(F32)).astype(BF16)
        r4[k] = [send(W.at[k, zidx(m8(z + d))], ZR.at[k, d - 1], at_z(d)) for d in range(1, 8)]
    for d in (1, 2, 3):
        recv(gy[d - 1], GY.at[m4(y - d)])
    GZ[zz] = GY[0] + GY[1] + GY[2] + GY[3]
    gz = [send(GZ.at[zz], GZ.at[zz], at_z(d)) for d in range(1, 8)]
    for k in range(2):
        for d in range(1, 8):
            recv(r4[k][d - 1], ZR.at[k, d - 1])
        got = W[k, zz].astype(F32)
        for d in range(7):
            got = got + ZR[k, d].astype(F32)
        NG[:, k * 128 : k * 128 + 128] = got

    own = pl.ds(pl.multiple_of(dp * 32, 32), 32)
    inv = INVS[own, 0:1]
    ng = NG[...]
    rows = AS[0:32, :]
    gain = AS[32:33, :]
    scaled = ng * gain
    for d in range(1, 8):
        recv(gz[d - 1], GZ.at[zidx(m8(z - d))])
    total = GZ[0]
    for i in range(1, 8):
        total = total + GZ[i]
    GT[...] = total
    wide = jnp.broadcast_to(GT[pl.ds(8 + y, 1)], (32, 128))
    inner = jnp.sum(jnp.where(lane == sub + zh * 32, wide, 0.0), axis=1, keepdims=True) / DS
    out = inv * scaled - rows * (inv * inv) * inner
    rows_o[...] = pltpu.roll(out, 224, 1)[:, 0:WS]
    at = (zl * 2 + c) * 2
    sums = jnp.concatenate([GT[pl.ds(at, 1)], GT[pl.ds(at + 1, 1)]], axis=1)
    sums = sums / jnp.where(lane_iota((1, 256)) < 32, 1.0, gain)
    gain_o[...] = pltpu.roll(jnp.broadcast_to(sums, (8, 256)), 224, 1)[0:1, 0:WS]
    for cp in sent:
        cp.wait_send()


def hand_over(gain_i, rows_i, hg_i, gain_o, rows_o, hg_o, sem):
    copies = [pltpu.make_async_copy(gain_i, gain_o, sem.at[4]), pltpu.make_async_copy(rows_i, rows_o, sem.at[5])]
    for i in range(4):
        part = pl.ds(i * 896, 896)
        copies.append(pltpu.make_async_copy(hg_i.at[part], hg_o.at[part], sem.at[i]))
    for cp in copies:
        cp.start()
    for cp in copies:
        cp.wait()


def local(teacher_rows, student_rows, teacher_gain, student_gain, teacher_head, student_head, labels):
    vmem = pl.BlockSpec(memory_space=pltpu.VMEM)
    anyw = pl.BlockSpec(memory_space=pl.ANY)
    hbm = pl.BlockSpec(memory_space=pltpu.HBM)
    V = pltpu.VMEM
    loss, gain_grad, rows_grad, head_grad = pl.pallas_call(
        kernel,
        out_shape=(
            jax.ShapeDtypeStruct((1, 1), F32),
            jax.ShapeDtypeStruct((1, WS), F32),
            jax.ShapeDtypeStruct((32, WS), F32),
            jax.ShapeDtypeStruct((DS, 512), BF16),
        ),
        in_specs=[hbm] * 7,
        out_specs=(vmem, vmem, vmem, vmem),
        scratch_shapes=[
            V((4, 4, 2, 4, 8, 32, 128), BF16),
            V((16, 256, 512), BF16),
            V((16, 128, 512), BF16),
            V((16, 256, 512), BF16),
            V((512, 4096), BF16),
            V((512, 512), F32), V((512, 512), F32), V((512, 512), F32),
            V((4, 512, 256), BF16), V((16, 512, 256), BF16),
            V((512, 512), BF16),
            V((512, 512), F32),
            V((40, 384), F32), V((40, 256), F32),
            V((512, 128), F32), V((512, 128), F32), V((512, 128), F32), V((512, 128), F32),
            V((128, 128), F32),
            V((8, 8, 128), F32), V((2, 16, 128), F32), V((4, 24, 128), F32), V((4, 8, 128), F32),
            V((2, 16, 128), F32), V((4, 16, 128), F32), V((4, 16, 128), F32), V((8, 16, 128), F32),
            V((2, 4, 4, 8, 32, 128), BF16), V((2, 4, 4, 8, 32, 128), BF16), V((2, 4, 4, 8, 32, 128), BF16),
            V((2, 2, 2, 8, 32, 128), BF16), V((2, 2, 4, 8, 32, 128), BF16),
            V((2, 4, 8, 32, 128), BF16), V((2, 3, 8, 32, 128), BF16),
            V((2, 8, 32, 128), BF16), V((2, 7, 32, 128), BF16),
            V((32, 256), F32),
            V((2, 40, 128), F32), V((4, 16, 128), F32), V((4, 16, 128), F32),
            V((4, 16, 128), F32), V((8, 16, 128), F32), V((16, 128), F32),
            V((32, WT), BF16), V((32, WS), BF16), V((WT,), BF16), V((WS,), BF16), V((4, 128), jnp.int32),
            pltpu.SemaphoreType.DMA((5,)),
            pltpu.SemaphoreType.DMA((3, 16)),
            pltpu.SemaphoreType.DMA((NSEM,)),
            pltpu.SemaphoreType.DMA((NSEM,)),
        ],
        compiler_params=pltpu.CompilerParams(
            collective_id=0, has_side_effects=True, vmem_limit_bytes=47 << 20
        ),
    )(
        teacher_rows, student_rows, teacher_gain, student_gain,
        labels.reshape(4, 128), teacher_head, student_head,
    )
    gain_grad, rows_grad, head_grad = pl.pallas_call(
        hand_over,
        out_shape=(
            jax.ShapeDtypeStruct((1, WS), F32),
            jax.ShapeDtypeStruct((32, WS), F32),
            jax.ShapeDtypeStruct((DS, 512), BF16),
        ),
        in_specs=[anyw] * 3,
        out_specs=(hbm, hbm, hbm),
        scratch_shapes=[pltpu.SemaphoreType.DMA((6,))],
        compiler_params=pltpu.CompilerParams(vmem_limit_bytes=8 << 20),
    )(gain_grad, rows_grad, head_grad)
    return loss.reshape(()), head_grad, gain_grad.reshape(WS), rows_grad


def solution(mesh):
    in_specs = (
        P("dp", "vocab"),
        P("dp", "vocab"),
        P("vocab"),
        P("vocab"),
        P(None, ("dp", "vocab")),
        P(None, ("dp", "vocab")),
        P(),
    )
    out_specs = (P(), P(None, ("dp", "vocab")), P("vocab"), P("dp", "vocab"))
    return jax.shard_map(local, mesh=mesh, in_specs=in_specs, out_specs=out_specs, check_vma=False)
```

```python
import functools

import jax
import jax.numpy as jnp
from jax import lax
from jax.experimental import pallas as pl
from jax.experimental.pallas import tpu as pltpu
from jax.sharding import PartitionSpec as P

MESH = pl.DeviceIdType.MESH
F32 = jnp.float32
BF16 = jnp.bfloat16
DT = 4608
DS = 3584
TOKENS = 512
CAP = 30.0
SCALE = 4096.0
EPS = 1e-06
WT = 288
WS = 224
NSEM = 160


def row_iota(shape):
    return lax.broadcasted_iota(jnp.int32, shape, 0)


def lane_iota(shape):
    return lax.broadcasted_iota(jnp.int32, shape, 1)


def kernel(
    tr_h, sr_h, tg_h, sg_h, lab_h, th, sh,
    loss_o, gain_o, rows_o, hg_o,
    G, TA, TB, SP, SPT, accT, accS, accA, NT, NS, gl, accZ,
    AT, AS, INVT, INVS, ST, LAB, SQ,
    MZ, MC, MX, MY, TC, TX, TY, TZ,
    PS, PR, R, RH, RB, Q, QR, W, ZR, NG,
    GI, GX, GXR, GY, GZ, GT,
    tr, sr, tg, sg, lab, isem, hsem, ssem, rsem,
):
    dp = lax.axis_index("dp")
    vo = lax.axis_index("vocab")
    y, zh = dp // 4, dp % 4
    x, zl, c = vo // 4, (vo // 2) % 2, vo % 2
    z = zh * 2 + zl
    zz = zl * 4 + zh
    pc = 1 - c

    def dev(x_, y_, z_, c_):
        return (y_ * 4 + z_ // 2, x_ * 4 + (z_ % 2) * 2 + c_)

    def m4(v):
        return lax.rem(v + 8, 4)

    def m8(v):
        return lax.rem(v + 16, 8)

    def at_x(d):
        return dev(m4(x + d), y, z, c)

    def at_y(d):
        return dev(x, m4(y + d), z, c)

    def at_z(d):
        return dev(x, y, m8(z + d), c)

    partner = dev(x, y, z, pc)

    def zidx(z_):
        return (z_ % 2) * 4 + z_ // 2

    count = [0]
    sent = []

    def send(src, dst, device):
        n = count[0]
        count[0] += 1
        cp = pltpu.make_async_remote_copy(
            src_ref=src, dst_ref=dst, send_sem=ssem.at[n], recv_sem=rsem.at[n],
            device_id=device, device_id_type=MESH,
        )
        cp.start()
        sent.append(cp)
        return n

    def recv(n, landing):
        pltpu.make_async_remote_copy(
            src_ref=landing, dst_ref=landing, send_sem=ssem.at[n], recv_sem=rsem.at[n],
            device_id=partner, device_id_type=MESH,
        ).wait_recv()

    def head_copies(v):
        v = jnp.int32(v)
        return (
            pltpu.make_async_copy(th.at[pl.ds(pl.multiple_of(v * WT, 16), 256)], TA.at[v], hsem.at[0, v]),
            pltpu.make_async_copy(th.at[pl.ds(pl.multiple_of(v * WT + 256, 16), 32)], TB.at[v, pl.ds(0, 32)], hsem.at[1, v]),
            pltpu.make_async_copy(sh.at[pl.ds(pl.multiple_of(v * WS, 16), WS)], SP.at[v, pl.ds(32, WS)], hsem.at[2, v]),
        )

    def wait_heads(v, _):
        for cp in head_copies(v):
            cp.wait()
        return 0

    own_copies = [
        pltpu.make_async_copy(src, dst, isem.at[i])
        for i, (src, dst) in enumerate(((tr_h, tr), (sr_h, sr), (tg_h, tg), (sg_h, sg), (lab_h, lab)))
    ]
    for cp in own_copies:
        cp.start()
    barrier = pltpu.get_barrier_semaphore()
    others = [partner] + [at_x(d) for d in (1, 2, 3)] + [at_y(d) for d in (1, 2, 3)] + [at_z(d) for d in range(1, 8)]
    for d in others:
        pl.semaphore_signal(barrier, inc=1, device_id=d, device_id_type=MESH)

    AT[...] = jnp.zeros_like(AT)
    AS[...] = jnp.zeros_like(AS)
    for cp in own_copies:
        cp.wait()
    AT[0:32, 0:WT] = tr[...].astype(F32)
    AS[0:32, 0:WS] = sr[...].astype(F32)
    AT[32:40, 0:WT] = jnp.broadcast_to(tg[...].astype(F32).reshape(1, WT), (8, WT))
    AS[32:40, 0:WS] = jnp.broadcast_to(sg[...].astype(F32).reshape(1, WS), (8, WS))
    a_t = AT[...]
    a_s = pltpu.roll(AS[...], 32, 1)
    AS[...] = a_s
    tiles = [a_t[:, 0:128], a_t[:, 128:256], a_t[:, 256:384] + a_s[:, 0:128], a_s[:, 128:256]]
    for j in range(4):
        b, o = (x, y) if j < 2 else (y, x)
        G[j, b, c, o, zz] = tiles[j][0:32].astype(BF16)
    sq_t = jnp.sum(a_t[0:32] * a_t[0:32], axis=1, keepdims=True)
    sq_s = jnp.sum(a_s[0:32] * a_s[0:32], axis=1, keepdims=True)
    sub, lane = row_iota((32, 128)), lane_iota((32, 128))
    MZ[zz] = jnp.zeros((8, 128), F32)
    MZ[zz, 0:1] = jnp.sum(jnp.where(lane == sub, sq_t, 0.0) + jnp.where(lane == sub + 32, sq_s, 0.0), axis=0, keepdims=True)
    for j in range(4):
        MZ[zz, 4 + j : 5 + j] = tiles[j][32:33]

    pl.semaphore_wait(barrier, len(others))

    mz = [send(MZ.at[zz], MZ.at[zz], at_z(d)) for d in range(1, 8)]
    zs = {}

    def z_send(j):
        b, o = (x, y) if j < 2 else (y, x)
        piece = G.at[j, b, c, o, zz]
        zs[j] = [send(piece, piece, at_z(d)) for d in range(1, 8)]

    z_send(0)
    z_send(2)

    def start_heads(v, _):
        for cp in head_copies(v):
            cp.start()
        return 0

    lax.fori_loop(0, 16, start_heads, 0)
    TB[:, 32:128, :] = jnp.zeros((16, 96, 512), BF16)
    SP[:, 0:32, :] = jnp.zeros((16, 32, 512), BF16)
    accT[...] = jnp.zeros_like(accT)
    accS[...] = jnp.zeros_like(accS)

    def axes(j):
        return (x, y, at_x, at_y) if j < 2 else (y, x, at_y, at_x)

    o1, o2, b1, b2, ds = {}, {}, {}, {}, {}

    def z_done(j):
        b, o, at_b, at_o = axes(j)
        for d in range(1, 8):
            recv(zs[j][d - 1], G.at[j, b, c, o, zidx(m8(z - d))])
        block = G.at[j, b, c, o]
        if j in (0, 2):
            o1[j] = [send(block, block, at_o(d)) for d in (1, 2, 3)]
        else:
            o1[j] = [send(block, block, at_o(1)), send(block, block, at_o(-1))]

    def o_near(j):
        b, o, at_b, at_o = axes(j)
        recv(o1[j][0], G.at[j, b, c, m4(o - 1)])
        half = G.at[j, b, c, m4(o - 1), pl.ds(0, 4)]
        f0 = send(half, half, at_o(1))
        recv(o1[j][1], G.at[j, b, c, m4(o + 1)])
        half = G.at[j, b, c, m4(o + 1), pl.ds(4, 4)]
        o2[j] = [f0, send(half, half, at_o(-1))]

    def o_far(j):
        b, o, at_b, at_o = axes(j)
        if j in (0, 2):
            for d in (1, 2, 3):
                recv(o1[j][d - 1], G.at[j, b, c, m4(o - d)])
        else:
            recv(o2[j][0], G.at[j, b, c, m4(o + 2), pl.ds(0, 4)])
            recv(o2[j][1], G.at[j, b, c, m4(o + 2), pl.ds(4, 4)])
        block = G.at[j, b, c]
        b1[j] = [send(block, block, at_b(1)), send(block, block, at_b(-1))]
        ds[j] = [send(block, block, partner)]

    def b_near(j):
        b, o, at_b, at_o = axes(j)
        recv(b1[j][0], G.at[j, m4(b - 1), c])
        half = G.at[j, m4(b - 1), c, pl.ds(0, 2)]
        f0 = send(half, half, at_b(1))
        recv(b1[j][1], G.at[j, m4(b + 1), c])
        half = G.at[j, m4(b + 1), c, pl.ds(2, 2)]
        b2[j] = [f0, send(half, half, at_b(-1))]
        for e in (-1, 1):
            block = G.at[j, m4(b + e), c]
            ds[j].append(send(block, block, partner))

    def b_far(j):
        b, o, at_b, at_o = axes(j)
        far = m4(b + 2)
        recv(b2[j][0], G.at[j, far, c, pl.ds(0, 2)])
        recv(b2[j][1], G.at[j, far, c, pl.ds(2, 2)])
        ds[j].append(send(G.at[j, far, c], G.at[j, far, c], partner))

    def core_done(j, ks):
        b = x if j < 2 else y
        for k in ks:
            recv(ds[j][k], G.at[j, m4(b + (0, -1, 1, 2)[k]), pc])

    z_done(0)
    z_done(2)
    z_send(1)
    z_send(3)
    for d in range(1, 8):
        recv(mz[d - 1], MZ.at[zidx(m8(z - d))])
    MC[c] = jnp.zeros((16, 128), F32)
    for h in range(4):
        MC[c, h : h + 1] = MZ[h, 0:1] + MZ[4 + h, 0:1]
    MC[c, 8:12] = MZ[zh, 4:8]
    MC[c, 12:16] = MZ[4 + zh, 4:8]
    mc = send(MC.at[c], MC.at[c], partner)
    recv(mc, MC.at[pc])
    MX[x] = jnp.zeros((24, 128), F32)
    MX[x, 0:8] = MC[0, 0:8] + MC[1, 0:8]
    MX[x, 8:16] = MC[0, 8:16]
    MX[x, 16:24] = MC[1, 8:16]
    mx = [send(MX.at[x], MX.at[x], at_x(d)) for d in (1, 2, 3)]
    o_far(0)
    o_far(2)
    z_done(1)
    z_done(3)
    for d in (1, 2, 3):
        recv(mx[d - 1], MX.at[m4(x - d)])
    MY[y] = MX[0, 0:8] + MX[1, 0:8] + MX[2, 0:8] + MX[3, 0:8]
    my = [send(MY.at[y], MY.at[y], at_y(d)) for d in (1, 2, 3)]
    o_near(1)
    o_near(3)
    o_far(1)
    o_far(3)
    for d in (1, 2, 3):
        recv(my[d - 1], MY.at[m4(y - d)])
    lane1 = lane_iota((8, 128))
    for yy in range(4):
        sums = MY[yy]
        inv = lax.rsqrt(jnp.where(lane1 < 32, sums / DT, sums / DS) + EPS)
        for h in range(4):
            wide = jnp.broadcast_to(inv[h : h + 1], (32, 128))
            base = (yy * 4 + h) * 32
            INVT[base : base + 32, :] = jnp.broadcast_to(jnp.sum(jnp.where(lane == sub, wide, 0.0), axis=1, keepdims=True), (32, 128))
            INVS[base : base + 32, :] = jnp.broadcast_to(jnp.sum(jnp.where(lane == sub + 32, wide, 0.0), axis=1, keepdims=True), (32, 128))
    sub2, lane2 = row_iota((128, 128)), lane_iota((128, 128))
    for blk in range(4):
        wide = jnp.broadcast_to(lab[blk : blk + 1, :].astype(F32), (128, 128))
        LAB[blk * 128 : blk * 128 + 128, :] = jnp.broadcast_to(jnp.sum(jnp.where(lane2 == sub2, wide, 0.0), axis=1, keepdims=True), (128, 128))
    lax.fori_loop(0, 16, wait_heads, 0)

    def teacher_block(x_):
        def norm(u, _):
            zl_, c_ = u // 2, u % 2
            for j in range(2):
                gain = MX[x_, pl.ds(8 + c_ * 8 + zl_ * 4 + j, 1)]
                for o_ in range(4):
                    rows = G[j, x_, c_, o_, pl.ds(zl_ * 4, 4)].reshape(128, 128).astype(F32)
                    r = rows * INVT[o_ * 128 : o_ * 128 + 128, :] * gain
                    NT[u, o_ * 128 : o_ * 128 + 128, j * 128 : j * 128 + 128] = r.astype(BF16)
            return 0

        lax.fori_loop(0, 4, norm, 0)

        def mul(n, _):
            cols = pl.ds(pl.multiple_of(n * 256, 256), 256)
            lt = jnp.concatenate([NT[u] for u in range(4)], axis=1)
            rt = jnp.concatenate([TA[x_ * 4 + u, :, cols] for u in range(4)], axis=0)
            accT[:, cols] += jnp.dot(lt, rt, preferred_element_type=F32)
            return 0

        lax.fori_loop(0, 2, mul, 0)

    def student_norm(y_):
        tok = pl.ds(pl.multiple_of(y_ * 128, 128), 128)

        def norm(v, _):
            x_, zl_, c_ = v // 4, (v // 2) % 2, v % 2
            for j in range(2):
                gain = MX[x_, pl.ds(8 + c_ * 8 + zl_ * 4 + 2 + j, 1)]
                rows = G[2 + j, y_, c_, x_, pl.ds(zl_ * 4, 4)].reshape(128, 128).astype(F32)
                inv = INVS[tok, :]
                if j == 0:
                    inv = jnp.where(lane2 < 32, INVT[tok, :], inv)
                NS[v, tok, j * 128 : j * 128 + 128] = (rows * inv * gain).astype(BF16)
            return 0

        lax.fori_loop(0, 16, norm, 0)

    def student_block(ys):
        toks = [pl.ds(pl.multiple_of(y_ * 128, 128), 128) for y_ in ys]

        def lhs(q, width):
            return jnp.concatenate(
                [jnp.concatenate([NS[q * 4 + u, tok, 0:width] for u in range(4)], axis=1) for tok in toks], axis=0
            )

        def mul(q, _):
            rs = jnp.concatenate([SP[q * 4 + u] for u in range(4)], axis=0)
            rb = jnp.concatenate([TB[q * 4 + u] for u in range(4)], axis=0)
            s_part = jnp.dot(lhs(q, 256), rs, preferred_element_type=F32)
            t_part = jnp.dot(lhs(q, 128), rb, preferred_element_type=F32)
            for i, tok in enumerate(toks):
                accS[tok, :] += s_part[i * 128 : i * 128 + 128]
                accT[tok, :] += t_part[i * 128 : i * 128 + 128]
            return 0

        lax.fori_loop(0, 4, mul, 0)

    def flip(v, _):
        SPT[:, pl.ds(pl.multiple_of(v * 256, 256), 256)] = jnp.transpose(SP[v])
        return 0

    for j in range(4):
        core_done(j, (0,))
    teacher_block(x)
    student_norm(y)
    b_near(0)
    b_near(2)
    student_block([y])
    b_near(1)
    b_near(3)
    for j in (0, 1):
        core_done(j, (1, 2))

    def teacher_near(i, _):
        teacher_block(m4(x - 1 + 2 * i))
        return 0

    def student_near(i, _):
        student_norm(m4(y - 1 + 2 * i))
        return 0

    lax.fori_loop(0, 2, teacher_near, 0)
    b_far(0)
    b_far(2)
    for j in (2, 3):
        core_done(j, (1, 2))
    lax.fori_loop(0, 2, student_near, 0)
    b_far(1)
    b_far(3)
    student_block([m4(y - 1), m4(y + 1)])
    for j in range(4):
        core_done(j, (3,))
    teacher_block(m4(x + 2))
    student_norm(m4(y + 2))
    student_block([m4(y + 2)])

    first = (dp * 16 + vo) * 512

    def stats(i, _):
        rows = pl.ds(pl.multiple_of(i * 64, 64), 64)
        tl = CAP * jnp.tanh(accT[rows, :] / CAP)
        sl = CAP * jnp.tanh(accS[rows, :] / CAP)
        et, es = jnp.exp(tl), jnp.exp(sl)
        want = LAB[rows, 0:1]
        hit = (lane_iota((64, 512)) + first).astype(F32) == want
        picked = jnp.sum(jnp.where(hit, sl, 0.0), axis=1, keepdims=True)
        cross = jnp.sum(et * (tl - sl), axis=1, keepdims=True)
        tot_t = jnp.sum(et, axis=1, keepdims=True)
        tot_s = jnp.sum(es, axis=1, keepdims=True)
        ln = lane_iota((64, 128))
        ST[rows, :] = jnp.where(ln == 0, tot_t, jnp.where(ln == 1, tot_s, jnp.where(ln == 2, cross, jnp.where(ln == 3, picked, 0.0))))
        accZ[rows, :] = accS[rows, :]
        slope = SCALE * (1.0 - (sl / CAP) ** 2)
        accA[rows, :] = 1.5 * es * slope
        accT[rows, :] = et * slope
        accS[rows, :] = jnp.where(hit, 0.5 * slope, 0.0)
        return 0

    lax.fori_loop(0, 8, stats, 0)
    for blk in range(4):
        t = jnp.transpose(ST[blk * 128 : blk * 128 + 128, :])
        for q in range(4):
            TC[c, q * 4 + blk : q * 4 + blk + 1] = t[q : q + 1]
    n = send(TC.at[c], TC.at[c], partner)
    recv(n, TC.at[pc])
    TX[x] = TC[0] + TC[1]
    ns = [send(TX.at[x], TX.at[x], at_x(d)) for d in (1, 2, 3)]
    lax.fori_loop(0, 8, flip, 0)
    for d in (1, 2, 3):
        recv(ns[d - 1], TX.at[m4(x - d)])
    TY[y] = TX[0] + TX[1] + TX[2] + TX[3]
    ns = [send(TY.at[y], TY.at[y], at_y(d)) for d in (1, 2, 3)]
    lax.fori_loop(8, 16, flip, 0)
    for d in (1, 2, 3):
        recv(ns[d - 1], TY.at[m4(y - d)])
    TZ[zz] = TY[0] + TY[1] + TY[2] + TY[3]
    ns = [send(TZ.at[zz], TZ.at[zz], at_z(d)) for d in range(1, 8)]
    for d in range(1, 8):
        recv(ns[d - 1], TZ.at[zidx(m8(z - d))])
    total = TZ[0]
    for i in range(1, 8):
        total = total + TZ[i]
    tt, ts, cr, pk = total[0:4], total[4:8], total[8:12], total[12:16]
    ls = jnp.log(ts)
    token_loss = cr / tt - jnp.log(tt) + ls + 0.5 * (ls - pk)
    loss_o[...] = jnp.sum(jnp.sum(token_loss, axis=1, keepdims=True), axis=0, keepdims=True) / TOKENS
    rec = 1.0 / total[0:8]
    SQ[...] = jnp.zeros_like(SQ)
    for blk in range(4):
        SQ[0:1, :] = rec[blk : blk + 1]
        SQ[1:2, :] = rec[4 + blk : 5 + blk]
        ST[blk * 128 : blk * 128 + 128, :] = jnp.transpose(SQ[...])

    def grads(i, _):
        rows = pl.ds(pl.multiple_of(i * 64, 64), 64)
        g = (accA[rows, :] * ST[rows, 1:2] - accT[rows, :] * ST[rows, 0:1] - accS[rows, :]).astype(BF16)
        gl[rows, :] = g
        dots = jnp.sum(g.astype(F32) * accZ[rows, :], axis=1, keepdims=True)
        LAB[rows, :] = jnp.broadcast_to(dots, (64, 128))
        return 0

    lax.fori_loop(0, 8, grads, 0)

    def as_row(column):
        return jnp.sum(jnp.where(lane2 == sub2, column, 0.0), axis=0, keepdims=True)

    def partial(v):
        return jnp.dot(gl[...], SPT[:, pl.ds(pl.multiple_of(v * 256, 256), 256)], preferred_element_type=F32).astype(BF16)

    def share(dst, x_, c_):
        def one(zl_, _):
            out = partial(x_ * 4 + zl_ * 2 + c_)
            for y_ in range(4):
                part = out[y_ * 128 : y_ * 128 + 128]
                dst[0, x_, y_, pl.ds(zl_ * 4, 4)] = part[:, 0:128].reshape(4, 32, 128)
                dst[1, y_, x_, pl.ds(zl_ * 4, 4)] = part[:, 128:256].reshape(4, 32, 128)
            return 0

        lax.fori_loop(0, 2, one, 0)

    order = [m4(x + 2), m4(x + 1), m4(x - 1), x]
    ps = []
    for x_ in order:
        share(PS, x_, pc)
        ps.append((send(PS.at[0, x_], PR.at[0, x_], partner), send(PS.at[1, :, x_], PR.at[1, :, x_], partner)))
    r1 = {}
    for i, x_ in enumerate(order):
        share(R, x_, c)
        recv(ps[i][0], PR.at[0, x_])
        for o_ in range(4):
            R[0, x_, o_] = (R[0, x_, o_].astype(F32) + PR[0, x_, o_].astype(F32)).astype(BF16)
        recv(ps[i][1], PR.at[1, :, x_])
        for b_ in range(4):
            R[1, b_, x_] = (R[1, b_, x_].astype(F32) + PR[1, b_, x_].astype(F32)).astype(BF16)
        if i == 0:
            r1[0] = (
                send(R.at[0, x_, pl.ds(0, 2)], RH.at[0, 0], at_x(1)),
                send(R.at[0, x_, pl.ds(2, 2)], RH.at[0, 1], at_x(-1)),
            )
    far = m4(y + 2)
    r1[1] = (
        send(R.at[1, far, pl.ds(0, 2)], RH.at[1, 0], at_y(1)),
        send(R.at[1, far, pl.ds(2, 2)], RH.at[1, 1], at_y(-1)),
    )

    def head_grad(v, _):
        out = lax.dot_general(NS[v], gl[...], (((0,), (0,)), ((), ())), preferred_element_type=F32)
        hg_o[pl.ds(pl.multiple_of(v * WS, 16), WS), :] = out[32:256].astype(BF16)
        sums = jnp.sum(out * SP[v].astype(F32), axis=1, keepdims=True)
        for h in range(2):
            GI[c, pl.ds(2 * v + h, 1)] = as_row(sums[h * 128 : h * 128 + 128])
        return 0

    GI[c, 32:40] = jnp.zeros((8, 128), F32)
    for blk in range(4):
        GI[c, 32 + blk : 33 + blk] = as_row(LAB[blk * 128 : blk * 128 + 128, :])
    lax.fori_loop(0, 8, head_grad, 0)
    r2 = {}
    for k in range(2):
        b = x if k == 0 else y
        at_b = at_x if k == 0 else at_y
        recv(r1[k][0], RH.at[k, 0])
        for o_ in range(2):
            R[k, m4(b + 1), o_] = (R[k, m4(b + 1), o_].astype(F32) + RH[k, 0, o_].astype(F32)).astype(BF16)
        n0 = send(R.at[k, m4(b + 1)], RB.at[k, 0], at_b(1))
        recv(r1[k][1], RH.at[k, 1])
        for o_ in range(2):
            R[k, m4(b - 1), 2 + o_] = (R[k, m4(b - 1), 2 + o_].astype(F32) + RH[k, 1, o_].astype(F32)).astype(BF16)
        n1 = send(R.at[k, m4(b - 1)], RB.at[k, 1], at_b(-1))
        r2[k] = (n0, n1)
    lax.fori_loop(8, 16, head_grad, 0)
    gi = send(GI.at[c], GI.at[c], partner)
    recv(gi, GI.at[pc])
    for x_ in range(4):
        GX[x_, 0:8] = GI[0, 8 * x_ : 8 * x_ + 8] + GI[1, 8 * x_ : 8 * x_ + 8]
        GX[x_, 8:16] = GI[0, 32:40] + GI[1, 32:40]
    GXR[x] = GX[x]
    gx = [send(GX.at[m4(x + d)], GXR.at[x], at_x(d)) for d in (1, 2, 3)]
    r3 = {}
    for k in range(2):
        b, o = (x, y) if k == 0 else (y, x)
        at_o = at_y if k == 0 else at_x
        recv(r2[k][0], RB.at[k, 0])
        recv(r2[k][1], RB.at[k, 1])
        for o_ in range(4):
            Q[k, o_] = (R[k, b, o_].astype(F32) + RB[k, 0, o_].astype(F32) + RB[k, 1, o_].astype(F32)).astype(BF16)
        r3[k] = [send(Q.at[k, m4(o + d)], QR.at[k, d - 1], at_o(d)) for d in (1, 2, 3)]
    for d in (1, 2, 3):
        recv(gx[d - 1], GXR.at[m4(x - d)])
    GY[y] = GXR[0] + GXR[1] + GXR[2] + GXR[3]
    gy = [send(GY.at[y], GY.at[y], at_y(d)) for d in (1, 2, 3)]
    r4 = {}
    for k in range(2):
        o = y if k == 0 else x
        for d in (1, 2, 3):
            recv(r3[k][d - 1], QR.at[k, d - 1])
        W[k] = (Q[k, o].astype(F32) + QR[k, 0].astype(F32) + QR[k, 1].astype(F32) + QR[k, 2].astype(F32)).astype(BF16)
        r4[k] = [send(W.at[k, zidx(m8(z + d))], ZR.at[k, d - 1], at_z(d)) for d in range(1, 8)]
    for d in (1, 2, 3):
        recv(gy[d - 1], GY.at[m4(y - d)])
    GZ[zz] = GY[0] + GY[1] + GY[2] + GY[3]
    gz = [send(GZ.at[zz], GZ.at[zz], at_z(d)) for d in range(1, 8)]
    for k in range(2):
        for d in range(1, 8):
            recv(r4[k][d - 1], ZR.at[k, d - 1])
        got = W[k, zz].astype(F32)
        for d in range(7):
            got = got + ZR[k, d].astype(F32)
        NG[:, k * 128 : k * 128 + 128] = got

    own = pl.ds(pl.multiple_of(dp * 32, 32), 32)
    inv = INVS[own, 0:1]
    ng = NG[...]
    rows = AS[0:32, :]
    gain = AS[32:33, :]
    scaled = ng * gain
    for d in range(1, 8):
        recv(gz[d - 1], GZ.at[zidx(m8(z - d))])
    total = GZ[0]
    for i in range(1, 8):
        total = total + GZ[i]
    GT[...] = total
    wide = jnp.broadcast_to(GT[pl.ds(8 + y, 1)], (32, 128))
    inner = jnp.sum(jnp.where(lane == sub + zh * 32, wide, 0.0), axis=1, keepdims=True) / DS
    out = inv * scaled - rows * (inv * inv) * inner
    rows_o[...] = pltpu.roll(out, 224, 1)[:, 0:WS]
    at = (zl * 2 + c) * 2
    sums = jnp.concatenate([GT[pl.ds(at, 1)], GT[pl.ds(at + 1, 1)]], axis=1)
    sums = sums / jnp.where(lane_iota((1, 256)) < 32, 1.0, gain)
    gain_o[...] = pltpu.roll(jnp.broadcast_to(sums, (8, 256)), 224, 1)[0:1, 0:WS]
    for cp in sent:
        cp.wait_send()


def hand_over(gain_i, rows_i, hg_i, gain_o, rows_o, hg_o, sem):
    copies = [pltpu.make_async_copy(gain_i, gain_o, sem.at[4]), pltpu.make_async_copy(rows_i, rows_o, sem.at[5])]
    for i in range(4):
        part = pl.ds(i * 896, 896)
        copies.append(pltpu.make_async_copy(hg_i.at[part], hg_o.at[part], sem.at[i]))
    for cp in copies:
        cp.start()
    for cp in copies:
        cp.wait()


def local(teacher_rows, student_rows, teacher_gain, student_gain, teacher_head, student_head, labels):
    vmem = pl.BlockSpec(memory_space=pltpu.VMEM)
    anyw = pl.BlockSpec(memory_space=pl.ANY)
    hbm = pl.BlockSpec(memory_space=pltpu.HBM)
    V = pltpu.VMEM
    loss, gain_grad, rows_grad, head_grad = pl.pallas_call(
        kernel,
        out_shape=(
            jax.ShapeDtypeStruct((1, 1), F32),
            jax.ShapeDtypeStruct((1, WS), F32),
            jax.ShapeDtypeStruct((32, WS), F32),
            jax.ShapeDtypeStruct((DS, 512), BF16),
        ),
        in_specs=[hbm] * 7,
        out_specs=(vmem, vmem, vmem, vmem),
        scratch_shapes=[
            V((4, 4, 2, 4, 8, 32, 128), BF16),
            V((16, 256, 512), BF16),
            V((16, 128, 512), BF16),
            V((16, 256, 512), BF16),
            V((512, 4096), BF16),
            V((512, 512), F32), V((512, 512), F32), V((512, 512), F32),
            V((4, 512, 256), BF16), V((16, 512, 256), BF16),
            V((512, 512), BF16),
            V((512, 512), F32),
            V((40, 384), F32), V((40, 256), F32),
            V((512, 128), F32), V((512, 128), F32), V((512, 128), F32), V((512, 128), F32),
            V((128, 128), F32),
            V((8, 8, 128), F32), V((2, 16, 128), F32), V((4, 24, 128), F32), V((4, 8, 128), F32),
            V((2, 16, 128), F32), V((4, 16, 128), F32), V((4, 16, 128), F32), V((8, 16, 128), F32),
            V((2, 4, 4, 8, 32, 128), BF16), V((2, 4, 4, 8, 32, 128), BF16), V((2, 4, 4, 8, 32, 128), BF16),
            V((2, 2, 2, 8, 32, 128), BF16), V((2, 2, 4, 8, 32, 128), BF16),
            V((2, 4, 8, 32, 128), BF16), V((2, 3, 8, 32, 128), BF16),
            V((2, 8, 32, 128), BF16), V((2, 7, 32, 128), BF16),
            V((32, 256), F32),
            V((2, 40, 128), F32), V((4, 16, 128), F32), V((4, 16, 128), F32),
            V((4, 16, 128), F32), V((8, 16, 128), F32), V((16, 128), F32),
            V((32, WT), BF16), V((32, WS), BF16), V((WT,), BF16), V((WS,), BF16), V((4, 128), jnp.int32),
            pltpu.SemaphoreType.DMA((5,)),
            pltpu.SemaphoreType.DMA((3, 16)),
            pltpu.SemaphoreType.DMA((NSEM,)),
            pltpu.SemaphoreType.DMA((NSEM,)),
        ],
        compiler_params=pltpu.CompilerParams(
            collective_id=0, has_side_effects=True, vmem_limit_bytes=47 << 20
        ),
    )(
        teacher_rows, student_rows, teacher_gain, student_gain,
        labels.reshape(4, 128), teacher_head, student_head,
    )
    gain_grad, rows_grad, head_grad = pl.pallas_call(
        hand_over,
        out_shape=(
            jax.ShapeDtypeStruct((1, WS), F32),
            jax.ShapeDtypeStruct((32, WS), F32),
            jax.ShapeDtypeStruct((DS, 512), BF16),
        ),
        in_specs=[anyw] * 3,
        out_specs=(hbm, hbm, hbm),
        scratch_shapes=[pltpu.SemaphoreType.DMA((6,))],
        compiler_params=pltpu.CompilerParams(vmem_limit_bytes=8 << 20),
    )(gain_grad, rows_grad, head_grad)
    return loss.reshape(()), head_grad, gain_grad.reshape(WS), rows_grad


def solution(mesh):
    in_specs = (
        P("dp", "vocab"),
        P("dp", "vocab"),
        P("vocab"),
        P("vocab"),
        P(None, ("dp", "vocab")),
        P(None, ("dp", "vocab")),
        P(),
    )
    out_specs = (P(), P(None, ("dp", "vocab")), P("vocab"), P("dp", "vocab"))
    return jax.shard_map(local, mesh=mesh, in_specs=in_specs, out_specs=out_specs, check_vma=False)
```

```python
import functools

import jax
import jax.numpy as jnp
from jax import lax
from jax.experimental import pallas as pl
from jax.experimental.pallas import tpu as pltpu
from jax.sharding import PartitionSpec as P

MESH = pl.DeviceIdType.MESH
F32 = jnp.float32
BF16 = jnp.bfloat16
DT = 4608
DS = 3584
TOKENS = 512
CAP = 30.0
SCALE = 4096.0
EPS = 1e-06
WT = 288
WS = 224
NSEM = 160


def row_iota(shape):
    return lax.broadcasted_iota(jnp.int32, shape, 0)


def lane_iota(shape):
    return lax.broadcasted_iota(jnp.int32, shape, 1)


def kernel(
    tr_h, sr_h, tg_h, sg_h, lab_h, th, sh,
    loss_o, gain_o, rows_o, hg_o,
    G, TA, TB, SP, SPT, accT, accS, accA, NT, NS, gl, accZ,
    AT, AS, INVT, INVS, ST, LAB, SQ,
    MZ, MC, MX, MY, TC, TX, TY, TZ,
    PS, PR, R, RH, RB, Q, QR, W, ZR, NG,
    GI, GX, GXR, GY, GZ, GT,
    tr, sr, tg, sg, lab, isem, hsem, ssem, rsem,
):
    dp = lax.axis_index("dp")
    vo = lax.axis_index("vocab")
    y, zh = dp // 4, dp % 4
    x, zl, c = vo // 4, (vo // 2) % 2, vo % 2
    z = zh * 2 + zl
    zz = zl * 4 + zh
    pc = 1 - c

    def dev(x_, y_, z_, c_):
        return (y_ * 4 + z_ // 2, x_ * 4 + (z_ % 2) * 2 + c_)

    def m4(v):
        return lax.rem(v + 8, 4)

    def m8(v):
        return lax.rem(v + 16, 8)

    def at_x(d):
        return dev(m4(x + d), y, z, c)

    def at_y(d):
        return dev(x, m4(y + d), z, c)

    def at_z(d):
        return dev(x, y, m8(z + d), c)

    partner = dev(x, y, z, pc)

    def zidx(z_):
        return (z_ % 2) * 4 + z_ // 2

    count = [0]
    sent = []

    def send(src, dst, device):
        n = count[0]
        count[0] += 1
        cp = pltpu.make_async_remote_copy(
            src_ref=src, dst_ref=dst, send_sem=ssem.at[n], recv_sem=rsem.at[n],
            device_id=device, device_id_type=MESH,
        )
        cp.start()
        sent.append(cp)
        return n

    def recv(n, landing):
        pltpu.make_async_remote_copy(
            src_ref=landing, dst_ref=landing, send_sem=ssem.at[n], recv_sem=rsem.at[n],
            device_id=partner, device_id_type=MESH,
        ).wait_recv()

    def head_copies(v):
        v = jnp.int32(v)
        return (
            pltpu.make_async_copy(th.at[pl.ds(pl.multiple_of(v * WT, 16), 256)], TA.at[v], hsem.at[0, v]),
            pltpu.make_async_copy(th.at[pl.ds(pl.multiple_of(v * WT + 256, 16), 32)], TB.at[v, pl.ds(0, 32)], hsem.at[1, v]),
            pltpu.make_async_copy(sh.at[pl.ds(pl.multiple_of(v * WS, 16), WS)], SP.at[v, pl.ds(32, WS)], hsem.at[2, v]),
        )

    def wait_heads(v, _):
        for cp in head_copies(v):
            cp.wait()
        return 0

    own_copies = [
        pltpu.make_async_copy(src, dst, isem.at[i])
        for i, (src, dst) in enumerate(((tr_h, tr), (sr_h, sr), (tg_h, tg), (sg_h, sg), (lab_h, lab)))
    ]
    for cp in own_copies:
        cp.start()
    barrier = pltpu.get_barrier_semaphore()
    others = [partner] + [at_x(d) for d in (1, 2, 3)] + [at_y(d) for d in (1, 2, 3)] + [at_z(d) for d in range(1, 8)]
    for d in others:
        pl.semaphore_signal(barrier, inc=1, device_id=d, device_id_type=MESH)

    AT[...] = jnp.zeros_like(AT)
    AS[...] = jnp.zeros_like(AS)
    for cp in own_copies:
        cp.wait()
    AT[0:32, 0:WT] = tr[...].astype(F32)
    AS[0:32, 0:WS] = sr[...].astype(F32)
    AT[32:40, 0:WT] = jnp.broadcast_to(tg[...].astype(F32).reshape(1, WT), (8, WT))
    AS[32:40, 0:WS] = jnp.broadcast_to(sg[...].astype(F32).reshape(1, WS), (8, WS))
    a_t = AT[...]
    a_s = pltpu.roll(AS[...], 32, 1)
    AS[...] = a_s
    tiles = [a_t[:, 0:128], a_t[:, 128:256], a_t[:, 256:384] + a_s[:, 0:128], a_s[:, 128:256]]
    for j in range(4):
        b, o = (x, y) if j < 2 else (y, x)
        G[j, b, c, o, zz] = tiles[j][0:32].astype(BF16)
    sq_t = jnp.sum(a_t[0:32] * a_t[0:32], axis=1, keepdims=True)
    sq_s = jnp.sum(a_s[0:32] * a_s[0:32], axis=1, keepdims=True)
    sub, lane = row_iota((32, 128)), lane_iota((32, 128))
    MZ[zz] = jnp.zeros((8, 128), F32)
    MZ[zz, 0:1] = jnp.sum(jnp.where(lane == sub, sq_t, 0.0) + jnp.where(lane == sub + 32, sq_s, 0.0), axis=0, keepdims=True)
    for j in range(4):
        MZ[zz, 4 + j : 5 + j] = tiles[j][32:33]

    pl.semaphore_wait(barrier, len(others))

    mz = [send(MZ.at[zz], MZ.at[zz], at_z(d)) for d in range(1, 8)]
    zs = {}

    def z_send(j):
        b, o = (x, y) if j < 2 else (y, x)
        piece = G.at[j, b, c, o, zz]
        zs[j] = [send(piece, piece, at_z(d)) for d in range(1, 8)]

    z_send(0)
    z_send(2)

    def start_heads(v, _):
        for cp in head_copies(v):
            cp.start()
        return 0

    lax.fori_loop(0, 16, start_heads, 0)
    TB[:, 32:128, :] = jnp.zeros((16, 96, 512), BF16)
    SP[:, 0:32, :] = jnp.zeros((16, 32, 512), BF16)
    accT[...] = jnp.zeros_like(accT)
    accS[...] = jnp.zeros_like(accS)

    def axes(j):
        return (x, y, at_x, at_y) if j < 2 else (y, x, at_y, at_x)

    o1, o2, b1, b2, ds = {}, {}, {}, {}, {}

    def z_done(j):
        b, o, at_b, at_o = axes(j)
        for d in range(1, 8):
            recv(zs[j][d - 1], G.at[j, b, c, o, zidx(m8(z - d))])
        block = G.at[j, b, c, o]
        if j in (0, 2):
            o1[j] = [send(block, block, at_o(d)) for d in (1, 2, 3)]
        else:
            o1[j] = [send(block, block, at_o(1)), send(block, block, at_o(-1))]

    def o_near(j):
        b, o, at_b, at_o = axes(j)
        recv(o1[j][0], G.at[j, b, c, m4(o - 1)])
        half = G.at[j, b, c, m4(o - 1), pl.ds(0, 4)]
        f0 = send(half, half, at_o(1))
        recv(o1[j][1], G.at[j, b, c, m4(o + 1)])
        half = G.at[j, b, c, m4(o + 1), pl.ds(4, 4)]
        o2[j] = [f0, send(half, half, at_o(-1))]

    def o_far(j):
        b, o, at_b, at_o = axes(j)
        if j in (0, 2):
            for d in (1, 2, 3):
                recv(o1[j][d - 1], G.at[j, b, c, m4(o - d)])
        else:
            recv(o2[j][0], G.at[j, b, c, m4(o + 2), pl.ds(0, 4)])
            recv(o2[j][1], G.at[j, b, c, m4(o + 2), pl.ds(4, 4)])
        block = G.at[j, b, c]
        b1[j] = [send(block, block, at_b(1)), send(block, block, at_b(-1))]
        ds[j] = [send(block, block, partner)]

    def b_near(j):
        b, o, at_b, at_o = axes(j)
        recv(b1[j][0], G.at[j, m4(b - 1), c])
        half = G.at[j, m4(b - 1), c, pl.ds(0, 2)]
        f0 = send(half, half, at_b(1))
        recv(b1[j][1], G.at[j, m4(b + 1), c])
        half = G.at[j, m4(b + 1), c, pl.ds(2, 2)]
        b2[j] = [f0, send(half, half, at_b(-1))]
        for e in (-1, 1):
            block = G.at[j, m4(b + e), c]
            ds[j].append(send(block, block, partner))

    def b_far(j):
        b, o, at_b, at_o = axes(j)
        far = m4(b + 2)
        recv(b2[j][0], G.at[j, far, c, pl.ds(0, 2)])
        recv(b2[j][1], G.at[j, far, c, pl.ds(2, 2)])
        ds[j].append(send(G.at[j, far, c], G.at[j, far, c], partner))

    def core_done(j, ks):
        b = x if j < 2 else y
        for k in ks:
            recv(ds[j][k], G.at[j, m4(b + (0, -1, 1, 2)[k]), pc])

    z_done(0)
    z_done(2)
    z_send(1)
    z_send(3)
    for d in range(1, 8):
        recv(mz[d - 1], MZ.at[zidx(m8(z - d))])
    MC[c] = jnp.zeros((16, 128), F32)
    for h in range(4):
        MC[c, h : h + 1] = MZ[h, 0:1] + MZ[4 + h, 0:1]
    MC[c, 8:12] = MZ[zh, 4:8]
    MC[c, 12:16] = MZ[4 + zh, 4:8]
    mc = send(MC.at[c], MC.at[c], partner)
    recv(mc, MC.at[pc])
    MX[x] = jnp.zeros((24, 128), F32)
    MX[x, 0:8] = MC[0, 0:8] + MC[1, 0:8]
    MX[x, 8:16] = MC[0, 8:16]
    MX[x, 16:24] = MC[1, 8:16]
    mx = [send(MX.at[x], MX.at[x], at_x(d)) for d in (1, 2, 3)]
    o_far(0)
    o_far(2)
    z_done(1)
    z_done(3)
    for d in (1, 2, 3):
        recv(mx[d - 1], MX.at[m4(x - d)])
    MY[y] = MX[0, 0:8] + MX[1, 0:8] + MX[2, 0:8] + MX[3, 0:8]
    my = [send(MY.at[y], MY.at[y], at_y(d)) for d in (1, 2, 3)]
    o_near(1)
    o_near(3)
    o_far(1)
    o_far(3)
    for d in (1, 2, 3):
        recv(my[d - 1], MY.at[m4(y - d)])
    lane1 = lane_iota((8, 128))
    for yy in range(4):
        sums = MY[yy]
        inv = lax.rsqrt(jnp.where(lane1 < 32, sums / DT, sums / DS) + EPS)
        for h in range(4):
            wide = jnp.broadcast_to(inv[h : h + 1], (32, 128))
            base = (yy * 4 + h) * 32
            INVT[base : base + 32, :] = jnp.broadcast_to(jnp.sum(jnp.where(lane == sub, wide, 0.0), axis=1, keepdims=True), (32, 128))
            INVS[base : base + 32, :] = jnp.broadcast_to(jnp.sum(jnp.where(lane == sub + 32, wide, 0.0), axis=1, keepdims=True), (32, 128))
    sub2, lane2 = row_iota((128, 128)), lane_iota((128, 128))
    for blk in range(4):
        wide = jnp.broadcast_to(lab[blk : blk + 1, :].astype(F32), (128, 128))
        LAB[blk * 128 : blk * 128 + 128, :] = jnp.broadcast_to(jnp.sum(jnp.where(lane2 == sub2, wide, 0.0), axis=1, keepdims=True), (128, 128))
    lax.fori_loop(0, 16, wait_heads, 0)

    def teacher_block(x_):
        def norm(u, _):
            zl_, c_ = u // 2, u % 2
            for j in range(2):
                gain = MX[x_, pl.ds(8 + c_ * 8 + zl_ * 4 + j, 1)]
                for o_ in range(4):
                    rows = G[j, x_, c_, o_, pl.ds(zl_ * 4, 4)].reshape(128, 128).astype(F32)
                    r = rows * INVT[o_ * 128 : o_ * 128 + 128, :] * gain
                    NT[u, o_ * 128 : o_ * 128 + 128, j * 128 : j * 128 + 128] = r.astype(BF16)
            return 0

        lax.fori_loop(0, 4, norm, 0)

        def mul(n, _):
            cols = pl.ds(pl.multiple_of(n * 256, 256), 256)
            lt = jnp.concatenate([NT[u] for u in range(4)], axis=1)
            rt = jnp.concatenate([TA[x_ * 4 + u, :, cols] for u in range(4)], axis=0)
            accT[:, cols] += jnp.dot(lt, rt, preferred_element_type=F32)
            return 0

        lax.fori_loop(0, 2, mul, 0)

    def student_norm(y_):
        tok = pl.ds(pl.multiple_of(y_ * 128, 128), 128)

        def norm(v, _):
            x_, zl_, c_ = v // 4, (v // 2) % 2, v % 2
            for j in range(2):
                gain = MX[x_, pl.ds(8 + c_ * 8 + zl_ * 4 + 2 + j, 1)]
                rows = G[2 + j, y_, c_, x_, pl.ds(zl_ * 4, 4)].reshape(128, 128).astype(F32)
                inv = INVS[tok, :]
                if j == 0:
                    inv = jnp.where(lane2 < 32, INVT[tok, :], inv)
                NS[v, tok, j * 128 : j * 128 + 128] = (rows * inv * gain).astype(BF16)
            return 0

        lax.fori_loop(0, 16, norm, 0)

    def student_block(ys):
        toks = [pl.ds(pl.multiple_of(y_ * 128, 128), 128) for y_ in ys]

        def lhs(q, width):
            return jnp.concatenate(
                [jnp.concatenate([NS[q * 4 + u, tok, 0:width] for u in range(4)], axis=1) for tok in toks], axis=0
            )

        def mul(q, _):
            rs = jnp.concatenate([SP[q * 4 + u] for u in range(4)], axis=0)
            rb = jnp.concatenate([TB[q * 4 + u] for u in range(4)], axis=0)
            s_part = jnp.dot(lhs(q, 256), rs, preferred_element_type=F32)
            t_part = jnp.dot(lhs(q, 128), rb, preferred_element_type=F32)
            for i, tok in enumerate(toks):
                accS[tok, :] += s_part[i * 128 : i * 128 + 128]
                accT[tok, :] += t_part[i * 128 : i * 128 + 128]
            return 0

        lax.fori_loop(0, 4, mul, 0)

    def flip(v, _):
        SPT[:, pl.ds(pl.multiple_of(v * 256, 256), 256)] = jnp.transpose(SP[v])
        return 0

    for j in range(4):
        core_done(j, (0,))
    teacher_block(x)
    student_norm(y)
    b_near(0)
    b_near(2)
    student_block([y])
    b_near(1)
    b_near(3)
    for j in (0, 1):
        core_done(j, (1, 2))

    def teacher_near(i, _):
        teacher_block(m4(x - 1 + 2 * i))
        return 0

    def student_near(i, _):
        student_norm(m4(y - 1 + 2 * i))
        return 0

    lax.fori_loop(0, 2, teacher_near, 0)
    b_far(0)
    b_far(2)
    for j in (2, 3):
        core_done(j, (1, 2))
    lax.fori_loop(0, 2, student_near, 0)
    b_far(1)
    b_far(3)
    student_block([m4(y - 1), m4(y + 1)])
    for j in range(4):
        core_done(j, (3,))
    teacher_block(m4(x + 2))
    student_norm(m4(y + 2))
    student_block([m4(y + 2)])

    first = (dp * 16 + vo) * 512

    def stats(i, _):
        rows = pl.ds(pl.multiple_of(i * 64, 64), 64)
        tl = CAP * jnp.tanh(accT[rows, :] / CAP)
        sl = CAP * jnp.tanh(accS[rows, :] / CAP)
        et, es = jnp.exp(tl), jnp.exp(sl)
        want = LAB[rows, 0:1]
        hit = (lane_iota((64, 512)) + first).astype(F32) == want
        picked = jnp.sum(jnp.where(hit, sl, 0.0), axis=1, keepdims=True)
        cross = jnp.sum(et * (tl - sl), axis=1, keepdims=True)
        tot_t = jnp.sum(et, axis=1, keepdims=True)
        tot_s = jnp.sum(es, axis=1, keepdims=True)
        ln = lane_iota((64, 128))
        ST[rows, :] = jnp.where(ln == 0, tot_t, jnp.where(ln == 1, tot_s, jnp.where(ln == 2, cross, jnp.where(ln == 3, picked, 0.0))))
        accZ[rows, :] = accS[rows, :]
        slope = SCALE * (1.0 - (sl / CAP) ** 2)
        accA[rows, :] = 1.5 * es * slope
        accT[rows, :] = et * slope
        accS[rows, :] = jnp.where(hit, 0.5 * slope, 0.0)
        return 0

    lax.fori_loop(0, 8, stats, 0)
    for blk in range(4):
        t = jnp.transpose(ST[blk * 128 : blk * 128 + 128, :])
        for q in range(4):
            TC[c, q * 4 + blk : q * 4 + blk + 1] = t[q : q + 1]
    n = send(TC.at[c], TC.at[c], partner)
    recv(n, TC.at[pc])
    TX[x] = TC[0] + TC[1]
    ns = [send(TX.at[x], TX.at[x], at_x(d)) for d in (1, 2, 3)]
    lax.fori_loop(0, 8, flip, 0)
    for d in (1, 2, 3):
        recv(ns[d - 1], TX.at[m4(x - d)])
    TY[y] = TX[0] + TX[1] + TX[2] + TX[3]
    ns = [send(TY.at[y], TY.at[y], at_y(d)) for d in (1, 2, 3)]
    lax.fori_loop(8, 16, flip, 0)
    for d in (1, 2, 3):
        recv(ns[d - 1], TY.at[m4(y - d)])
    TZ[zz] = TY[0] + TY[1] + TY[2] + TY[3]
    ns = [send(TZ.at[zz], TZ.at[zz], at_z(d)) for d in range(1, 8)]
    for d in range(1, 8):
        recv(ns[d - 1], TZ.at[zidx(m8(z - d))])
    total = TZ[0]
    for i in range(1, 8):
        total = total + TZ[i]
    tt, ts, cr, pk = total[0:4], total[4:8], total[8:12], total[12:16]
    ls = jnp.log(ts)
    token_loss = cr / tt - jnp.log(tt) + ls + 0.5 * (ls - pk)
    loss_o[...] = jnp.sum(jnp.sum(token_loss, axis=1, keepdims=True), axis=0, keepdims=True) / TOKENS
    rec = 1.0 / total[0:8]
    SQ[...] = jnp.zeros_like(SQ)
    for blk in range(4):
        SQ[0:1, :] = rec[blk : blk + 1]
        SQ[1:2, :] = rec[4 + blk : 5 + blk]
        ST[blk * 128 : blk * 128 + 128, :] = jnp.transpose(SQ[...])

    def grads(i, _):
        rows = pl.ds(pl.multiple_of(i * 64, 64), 64)
        g = (accA[rows, :] * ST[rows, 1:2] - accT[rows, :] * ST[rows, 0:1] - accS[rows, :]).astype(BF16)
        gl[rows, :] = g
        dots = jnp.sum(g.astype(F32) * accZ[rows, :], axis=1, keepdims=True)
        LAB[rows, :] = jnp.broadcast_to(dots, (64, 128))
        return 0

    lax.fori_loop(0, 8, grads, 0)

    def as_row(column):
        return jnp.sum(jnp.where(lane2 == sub2, column, 0.0), axis=0, keepdims=True)

    def partial(v):
        return jnp.dot(gl[...], SPT[:, pl.ds(pl.multiple_of(v * 256, 256), 256)], preferred_element_type=F32).astype(BF16)

    def share(dst, x_, c_):
        def one(zl_, _):
            out = partial(x_ * 4 + zl_ * 2 + c_)
            for y_ in range(4):
                part = out[y_ * 128 : y_ * 128 + 128]
                dst[0, x_, y_, pl.ds(zl_ * 4, 4)] = part[:, 0:128].reshape(4, 32, 128)
                dst[1, y_, x_, pl.ds(zl_ * 4, 4)] = part[:, 128:256].reshape(4, 32, 128)
            return 0

        lax.fori_loop(0, 2, one, 0)

    order = [m4(x + 2), m4(x + 1), m4(x - 1), x]
    ps = []
    for x_ in order:
        share(PS, x_, pc)
        ps.append((send(PS.at[0, x_], PR.at[0, x_], partner), send(PS.at[1, :, x_], PR.at[1, :, x_], partner)))
    r1 = {}
    for i, x_ in enumerate(order):
        share(R, x_, c)
        recv(ps[i][0], PR.at[0, x_])
        for o_ in range(4):
            R[0, x_, o_] = (R[0, x_, o_].astype(F32) + PR[0, x_, o_].astype(F32)).astype(BF16)
        recv(ps[i][1], PR.at[1, :, x_])
        for b_ in range(4):
            R[1, b_, x_] = (R[1, b_, x_].astype(F32) + PR[1, b_, x_].astype(F32)).astype(BF16)
        if i == 0:
            r1[0] = (
                send(R.at[0, x_, pl.ds(0, 2)], RH.at[0, 0], at_x(1)),
                send(R.at[0, x_, pl.ds(2, 2)], RH.at[0, 1], at_x(-1)),
            )
    far = m4(y + 2)
    r1[1] = (
        send(R.at[1, far, pl.ds(0, 2)], RH.at[1, 0], at_y(1)),
        send(R.at[1, far, pl.ds(2, 2)], RH.at[1, 1], at_y(-1)),
    )

    def head_grad(v, _):
        out = lax.dot_general(NS[v], gl[...], (((0,), (0,)), ((), ())), preferred_element_type=F32)
        hg_o[pl.ds(pl.multiple_of(v * WS, 16), WS), :] = out[32:256].astype(BF16)
        sums = jnp.sum(out * SP[v].astype(F32), axis=1, keepdims=True)
        for h in range(2):
            GI[c, pl.ds(2 * v + h, 1)] = as_row(sums[h * 128 : h * 128 + 128])
        return 0

    GI[c, 32:40] = jnp.zeros((8, 128), F32)
    for blk in range(4):
        GI[c, 32 + blk : 33 + blk] = as_row(LAB[blk * 128 : blk * 128 + 128, :])
    lax.fori_loop(0, 10, head_grad, 0)
    r2 = {}
    for k in range(2):
        b = x if k == 0 else y
        at_b = at_x if k == 0 else at_y
        recv(r1[k][0], RH.at[k, 0])
        for o_ in range(2):
            R[k, m4(b + 1), o_] = (R[k, m4(b + 1), o_].astype(F32) + RH[k, 0, o_].astype(F32)).astype(BF16)
        n0 = send(R.at[k, m4(b + 1)], RB.at[k, 0], at_b(1))
        recv(r1[k][1], RH.at[k, 1])
        for o_ in range(2):
            R[k, m4(b - 1), 2 + o_] = (R[k, m4(b - 1), 2 + o_].astype(F32) + RH[k, 1, o_].astype(F32)).astype(BF16)
        n1 = send(R.at[k, m4(b - 1)], RB.at[k, 1], at_b(-1))
        r2[k] = (n0, n1)
    lax.fori_loop(10, 16, head_grad, 0)
    gi = send(GI.at[c], GI.at[c], partner)
    recv(gi, GI.at[pc])
    for x_ in range(4):
        GX[x_, 0:8] = GI[0, 8 * x_ : 8 * x_ + 8] + GI[1, 8 * x_ : 8 * x_ + 8]
        GX[x_, 8:16] = GI[0, 32:40] + GI[1, 32:40]
    GXR[x] = GX[x]
    gx = [send(GX.at[m4(x + d)], GXR.at[x], at_x(d)) for d in (1, 2, 3)]
    r3 = {}
    for k in range(2):
        b, o = (x, y) if k == 0 else (y, x)
        at_o = at_y if k == 0 else at_x
        recv(r2[k][0], RB.at[k, 0])
        recv(r2[k][1], RB.at[k, 1])
        for o_ in range(4):
            Q[k, o_] = (R[k, b, o_].astype(F32) + RB[k, 0, o_].astype(F32) + RB[k, 1, o_].astype(F32)).astype(BF16)
        r3[k] = [send(Q.at[k, m4(o + d)], QR.at[k, d - 1], at_o(d)) for d in (1, 2, 3)]
    for d in (1, 2, 3):
        recv(gx[d - 1], GXR.at[m4(x - d)])
    GY[y] = GXR[0] + GXR[1] + GXR[2] + GXR[3]
    gy = [send(GY.at[y], GY.at[y], at_y(d)) for d in (1, 2, 3)]
    r4 = {}
    for k in range(2):
        o = y if k == 0 else x
        for d in (1, 2, 3):
            recv(r3[k][d - 1], QR.at[k, d - 1])
        W[k] = (Q[k, o].astype(F32) + QR[k, 0].astype(F32) + QR[k, 1].astype(F32) + QR[k, 2].astype(F32)).astype(BF16)
        r4[k] = [send(W.at[k, zidx(m8(z + d))], ZR.at[k, d - 1], at_z(d)) for d in range(1, 8)]
    for d in (1, 2, 3):
        recv(gy[d - 1], GY.at[m4(y - d)])
    GZ[zz] = GY[0] + GY[1] + GY[2] + GY[3]
    gz = [send(GZ.at[zz], GZ.at[zz], at_z(d)) for d in range(1, 8)]
    for k in range(2):
        for d in range(1, 8):
            recv(r4[k][d - 1], ZR.at[k, d - 1])
        got = W[k, zz].astype(F32)
        for d in range(7):
            got = got + ZR[k, d].astype(F32)
        NG[:, k * 128 : k * 128 + 128] = got

    own = pl.ds(pl.multiple_of(dp * 32, 32), 32)
    inv = INVS[own, 0:1]
    ng = NG[...]
    rows = AS[0:32, :]
    gain = AS[32:33, :]
    scaled = ng * gain
    for d in range(1, 8):
        recv(gz[d - 1], GZ.at[zidx(m8(z - d))])
    total = GZ[0]
    for i in range(1, 8):
        total = total + GZ[i]
    GT[...] = total
    wide = jnp.broadcast_to(GT[pl.ds(8 + y, 1)], (32, 128))
    inner = jnp.sum(jnp.where(lane == sub + zh * 32, wide, 0.0), axis=1, keepdims=True) / DS
    out = inv * scaled - rows * (inv * inv) * inner
    rows_o[...] = pltpu.roll(out, 224, 1)[:, 0:WS]
    at = (zl * 2 + c) * 2
    sums = jnp.concatenate([GT[pl.ds(at, 1)], GT[pl.ds(at + 1, 1)]], axis=1)
    sums = sums / jnp.where(lane_iota((1, 256)) < 32, 1.0, gain)
    gain_o[...] = pltpu.roll(jnp.broadcast_to(sums, (8, 256)), 224, 1)[0:1, 0:WS]
    for cp in sent:
        cp.wait_send()


def hand_over(gain_i, rows_i, hg_i, gain_o, rows_o, hg_o, sem):
    copies = [pltpu.make_async_copy(gain_i, gain_o, sem.at[4]), pltpu.make_async_copy(rows_i, rows_o, sem.at[5])]
    for i in range(4):
        part = pl.ds(i * 896, 896)
        copies.append(pltpu.make_async_copy(hg_i.at[part], hg_o.at[part], sem.at[i]))
    for cp in copies:
        cp.start()
    for cp in copies:
        cp.wait()


def local(teacher_rows, student_rows, teacher_gain, student_gain, teacher_head, student_head, labels):
    vmem = pl.BlockSpec(memory_space=pltpu.VMEM)
    anyw = pl.BlockSpec(memory_space=pl.ANY)
    hbm = pl.BlockSpec(memory_space=pltpu.HBM)
    V = pltpu.VMEM
    loss, gain_grad, rows_grad, head_grad = pl.pallas_call(
        kernel,
        out_shape=(
            jax.ShapeDtypeStruct((1, 1), F32),
            jax.ShapeDtypeStruct((1, WS), F32),
            jax.ShapeDtypeStruct((32, WS), F32),
            jax.ShapeDtypeStruct((DS, 512), BF16),
        ),
        in_specs=[hbm] * 7,
        out_specs=(vmem, vmem, vmem, vmem),
        scratch_shapes=[
            V((4, 4, 2, 4, 8, 32, 128), BF16),
            V((16, 256, 512), BF16),
            V((16, 128, 512), BF16),
            V((16, 256, 512), BF16),
            V((512, 4096), BF16),
            V((512, 512), F32), V((512, 512), F32), V((512, 512), F32),
            V((4, 512, 256), BF16), V((16, 512, 256), BF16),
            V((512, 512), BF16),
            V((512, 512), F32),
            V((40, 384), F32), V((40, 256), F32),
            V((512, 128), F32), V((512, 128), F32), V((512, 128), F32), V((512, 128), F32),
            V((128, 128), F32),
            V((8, 8, 128), F32), V((2, 16, 128), F32), V((4, 24, 128), F32), V((4, 8, 128), F32),
            V((2, 16, 128), F32), V((4, 16, 128), F32), V((4, 16, 128), F32), V((8, 16, 128), F32),
            V((2, 4, 4, 8, 32, 128), BF16), V((2, 4, 4, 8, 32, 128), BF16), V((2, 4, 4, 8, 32, 128), BF16),
            V((2, 2, 2, 8, 32, 128), BF16), V((2, 2, 4, 8, 32, 128), BF16),
            V((2, 4, 8, 32, 128), BF16), V((2, 3, 8, 32, 128), BF16),
            V((2, 8, 32, 128), BF16), V((2, 7, 32, 128), BF16),
            V((32, 256), F32),
            V((2, 40, 128), F32), V((4, 16, 128), F32), V((4, 16, 128), F32),
            V((4, 16, 128), F32), V((8, 16, 128), F32), V((16, 128), F32),
            V((32, WT), BF16), V((32, WS), BF16), V((WT,), BF16), V((WS,), BF16), V((4, 128), jnp.int32),
            pltpu.SemaphoreType.DMA((5,)),
            pltpu.SemaphoreType.DMA((3, 16)),
            pltpu.SemaphoreType.DMA((NSEM,)),
            pltpu.SemaphoreType.DMA((NSEM,)),
        ],
        compiler_params=pltpu.CompilerParams(
            collective_id=0, has_side_effects=True, vmem_limit_bytes=47 << 20
        ),
    )(
        teacher_rows, student_rows, teacher_gain, student_gain,
        labels.reshape(4, 128), teacher_head, student_head,
    )
    gain_grad, rows_grad, head_grad = pl.pallas_call(
        hand_over,
        out_shape=(
            jax.ShapeDtypeStruct((1, WS), F32),
            jax.ShapeDtypeStruct((32, WS), F32),
            jax.ShapeDtypeStruct((DS, 512), BF16),
        ),
        in_specs=[anyw] * 3,
        out_specs=(hbm, hbm, hbm),
        scratch_shapes=[pltpu.SemaphoreType.DMA((6,))],
        compiler_params=pltpu.CompilerParams(vmem_limit_bytes=8 << 20),
    )(gain_grad, rows_grad, head_grad)
    return loss.reshape(()), head_grad, gain_grad.reshape(WS), rows_grad


def solution(mesh):
    in_specs = (
        P("dp", "vocab"),
        P("dp", "vocab"),
        P("vocab"),
        P("vocab"),
        P(None, ("dp", "vocab")),
        P(None, ("dp", "vocab")),
        P(),
    )
    out_specs = (P(), P(None, ("dp", "vocab")), P("vocab"), P("dp", "vocab"))
    return jax.shard_map(local, mesh=mesh, in_specs=in_specs, out_specs=out_specs, check_vma=False)
```
